512 devices in a mesh: rows: 64 (over z, y), cols: 8 (over x, core).
Axes of the slice: x: 4, y: 4, z: 16, core: 2. Of those that a mesh axis runs over, the one named last changes fastest.
Arguments:
- tile_blocks: bfloat16 [64, 64, 128, 128], P('rows', 'cols'), as said below
- tile_row: int32 [64, 64], P('rows', 'cols'), may hold values from 0 to 1, as said below
- tile_col: int32 [64, 64], P('rows', 'cols'), may hold values from 0 to 3, as said below
- tile_count: int32 [64, 8], P('rows', 'cols'), may hold values from 4 to 8, as said below
- column_costs: float32 [4096], P('cols'), may hold values from 0.5 to 2
- demand: int32 [16384, 256], P('rows'), may hold values from 0 to 7
- primal_start: float32 [4096, 256], P('cols'), may hold values from 0 to 0.5
- dual_start: float32 [16384, 256], P('rows'), may hold values from -6 to 6
Outputs:
- solution: float32 [4096, 256], P('cols')
- dual_values: float32 [16384, 256], P('rows')
- primal_residual: float32 [16384, 256], P('rows')
- primal_weight: float32 [256], replicated
The draws below stay inside these ranges and needn't reach their ends.
Inputs may be any that keep to these rules, and one draw needn't show every extreme that they name: Within one device the slots name distinct (tile_row, tile_col) pairs, all 8 of them; the first max(2, 4) slots name every block-row and every block-column of the device. `tile_col`: paired with tile_row slot by slot. `tile_count`: some device uses all 8 slots in every draw; only slots below a device's count hold blocks of A. `tile_blocks`: slots at or above a device's count hold values that are not part of A.
All inputs are finite; a program needn't handle non-finite values.
Results may differ from the reference program's by a relative error of at most 0.0003.
Values sent between devices are 32-bit elements; how exact they have to be, the bound alone decides.
A program may use at most 64 MiB of HBM per device.

```python
import math
from functools import partial
import jax
import jax.numpy as jnp
from jax import lax

ROW_BLOCKS = 2
COL_BLOCKS = 4
TILE = 128
SCENARIOS = 256
SWEEPS = 2
ITERS = 4
SLOTS = 8
DUALS = 16384
PRIMALS = 4096
N_ROWS = 64
N_COLS = 8


def tile_layout(key):
    base_key = jax.random.fold_in(key, 7)
    key_shift, key_order, key_count, key_busy = jax.random.split(base_key, 4)
    pair_total = ROW_BLOCKS * COL_BLOCKS
    cover_total = max(ROW_BLOCKS, COL_BLOCKS)
    shift = jax.random.randint(key_shift, (N_ROWS, N_COLS, 1), 0, ROW_BLOCKS)
    ranks = jnp.arange(cover_total, dtype=jnp.int32)[None, None, :]
    cover_ids = (ranks + shift) % ROW_BLOCKS * COL_BLOCKS + ranks % COL_BLOCKS
    pair_ids = jnp.arange(pair_total, dtype=jnp.int32)
    covered = jnp.sum((cover_ids[..., None] == pair_ids[None, None, None, :]).astype(jnp.int32), axis=2)
    jitter = jax.random.randint(key_order, (N_ROWS, N_COLS, pair_total), 0, 1 << 16)
    scores = (1 - covered) * (1 << 22) + jitter * pair_total + pair_ids[None, None, :]
    ordering = jnp.argsort(scores, axis=-1, stable=True).astype(jnp.int32)
    row_ids = (ordering // COL_BLOCKS).reshape(N_ROWS, N_COLS * pair_total)
    col_ids = (ordering % COL_BLOCKS).reshape(N_ROWS, N_COLS * pair_total)
    slot_counts = jax.random.randint(key_count, (N_ROWS * N_COLS,), cover_total, pair_total + 1)
    busiest = jax.random.randint(key_busy, (), 0, N_ROWS * N_COLS)
    slot_counts = jnp.where(jnp.arange(N_ROWS * N_COLS, dtype=jnp.int32) == busiest, pair_total, slot_counts)
    return (row_ids, col_ids, slot_counts.reshape(N_ROWS, N_COLS).astype(jnp.int32))


def draw_tile_row(key, part):
    return tile_layout(key)[0]


def draw_tile_col(key, part):
    return tile_layout(key)[1]


def draw_tile_count(key, part):
    return tile_layout(key)[2]


def draw_tile_blocks(key, part):
    key_values, key_rows, key_cols = jax.random.split(jax.random.fold_in(key, 11), 3)
    full_shape = (N_ROWS, N_COLS * SLOTS, TILE, TILE)
    values = jax.random.normal(key_values, full_shape, jnp.float32)
    lowest = 0.3
    row_factor = jnp.exp(jax.random.uniform(key_rows, (N_ROWS, N_COLS * SLOTS, TILE, 1), jnp.float32, math.log(lowest), math.log(3.0)))
    col_factor = jnp.exp(jax.random.uniform(key_cols, (N_ROWS, N_COLS * SLOTS, 1, TILE), jnp.float32, math.log(lowest), math.log(3.0)))
    return (values * row_factor * col_factor).astype(jnp.bfloat16)


def plant(array, rng, low, high):
    longest = array.shape.index(max(array.shape))
    spots = []
    for shift in (0, 1):
        where = [jax.random.randint(jax.random.fold_in(rng, axis), (), 0, length) for axis, length in enumerate(array.shape)]
        where[longest] = (where[longest] + shift) % array.shape[longest]
        spots.append(tuple(where))
    return array.at[spots[0]].set(low).at[spots[1]].set(high)


def steps_of(own_key, shape, cuts, smallest, high):
    def one(position, shards_of):
        heights = jax.random.uniform(jax.random.fold_in(jax.random.fold_in(own_key, 6), position), (shards_of,), jnp.float32, smallest / len(cuts), high / len(cuts))
        return jnp.repeat(jnp.exp(heights), shape[position] // shards_of).reshape((-1,) + (1,) * (len(shape) - position - 1))

    loudness = one(*cuts[0])
    for cut in cuts[1:]:
        loudness = loudness * one(*cut)
    return loudness


def normal_values(own_key, shape, width, reach, shards=(), kind=jnp.bfloat16):
    level = steps_of(own_key, shape, shards, -0.22, 0.18) if shards else 1.0
    array = jax.random.normal(own_key, shape, jnp.float32) * width * level
    return jnp.minimum(jnp.maximum(array, -reach), reach).astype(kind)


def setup_inputs(seed: int = 0) -> dict:
    keys = jax.random.split(jax.random.key(seed), 9)
    tile_blocks = draw_tile_blocks(jax.random.fold_in(keys[8], 71), 0)
    tile_row = draw_tile_row(jax.random.fold_in(keys[8], 71), 0)
    tile_col = draw_tile_col(jax.random.fold_in(keys[8], 71), 0)
    tile_count = draw_tile_count(jax.random.fold_in(keys[8], 71), 0)
    column_costs = jnp.clip(jnp.exp(math.log(2.0) - 1.3862944 * jax.random.uniform(keys[4], (PRIMALS,), jnp.float32) ** steps_of(keys[4], (PRIMALS,), ((0, 8),), -0.2, 0.2)), 0.5, 2.0)
    demand = plant(jax.random.randint(keys[5], (DUALS, SCENARIOS), 0, 8), jax.random.fold_in(keys[5], 1), 0, 7).astype(jnp.int32)
    primal_start = jnp.clip(0.5 * jax.random.uniform(keys[6], (PRIMALS, SCENARIOS), jnp.float32) ** steps_of(keys[6], (PRIMALS, SCENARIOS), ((0, 8),), -0.2, 0.2), 0.0, 0.5)
    dual_start = normal_values(keys[7], (DUALS, SCENARIOS), 1.0, 6.0, ((0, 64),), jnp.float32)
    return {"tile_blocks": tile_blocks, "tile_row": tile_row, "tile_col": tile_col, "tile_count": tile_count, "column_costs": column_costs, "demand": demand, "primal_start": primal_start, "dual_start": dual_start}


HIGHEST = lax.Precision.HIGHEST
EPSILON = 1e-06

def slot_tables(tile_row, tile_col, tile_count):
    live_mask = (jnp.arange(tile_row.shape[0], dtype=jnp.int32) < tile_count).astype(jnp.float32)
    row_hot = (tile_row[:, None] == jnp.arange(ROW_BLOCKS, dtype=jnp.int32)[None, :]).astype(jnp.float32) * live_mask[:, None]
    col_hot = (tile_col[:, None] == jnp.arange(COL_BLOCKS, dtype=jnp.int32)[None, :]).astype(jnp.float32) * live_mask[:, None]
    return (row_hot, col_hot)

def scaled_tiles(blocks, row_hot, col_hot, row_scale, col_scale):
    magnitude = jnp.abs(blocks.astype(jnp.float32))
    row_pick = jnp.einsum('tr,rk->tk', row_hot, row_scale, precision=HIGHEST)
    col_pick = jnp.einsum('tc,ck->tk', col_hot, col_scale, precision=HIGHEST)
    return magnitude * row_pick[:, :, None] * col_pick[:, None, :]

def extremes(scaled, row_hot, col_hot):
    row_part = lax.optimization_barrier(jnp.max(row_hot.T[:, :, None] * lax.optimization_barrier(jnp.max(scaled, axis=2))[None], axis=1))
    col_part = lax.optimization_barrier(jnp.max(col_hot.T[:, :, None] * lax.optimization_barrier(jnp.max(scaled, axis=1))[None], axis=1))
    return (row_part, col_part)

def totals(scaled, row_hot, col_hot):
    row_part = jnp.einsum('tr,tk->rk', row_hot, lax.optimization_barrier(jnp.sum(scaled, axis=2)), precision=HIGHEST)
    col_part = jnp.einsum('tc,tk->ck', col_hot, lax.optimization_barrier(jnp.sum(scaled, axis=1)), precision=HIGHEST)
    return (row_part, col_part)

def forward(blocks, row_hot, col_hot, vectors):
    picked = jnp.einsum('tc,cks->tks', col_hot, vectors, precision=HIGHEST)
    product = jnp.einsum('tij,tjs->tis', blocks.astype(jnp.float32), picked, precision=HIGHEST)
    return jnp.einsum('tr,tis->ris', row_hot, product, precision=HIGHEST)

def backward(blocks, row_hot, col_hot, vectors):
    picked = jnp.einsum('tr,rks->tks', row_hot, vectors, precision=HIGHEST)
    product = jnp.einsum('tij,tis->tjs', blocks.astype(jnp.float32), picked, precision=HIGHEST)
    return jnp.einsum('tc,tjs->cjs', col_hot, product, precision=HIGHEST)

def slab_extremes(pieces, col_scale):
    slab_blocks, slab_rows, slab_cols, slab_scale = pieces
    scaled = jax.vmap(scaled_tiles, in_axes=(0, 0, 0, None, 0))(slab_blocks, slab_rows, slab_cols, slab_scale, col_scale)
    row_part, col_part = jax.vmap(extremes)(scaled, slab_rows, slab_cols)
    return (lax.optimization_barrier(jnp.max(row_part, axis=0)), col_part)

def slab_totals(pieces, col_scale):
    slab_blocks, slab_rows, slab_cols, slab_scale = pieces
    scaled = jax.vmap(scaled_tiles, in_axes=(0, 0, 0, None, 0))(slab_blocks, slab_rows, slab_cols, slab_scale, col_scale)
    row_part, col_part = jax.vmap(totals)(scaled, slab_rows, slab_cols)
    return (lax.optimization_barrier(jnp.sum(row_part, axis=0)), col_part)

def slab_forward(pieces, vectors):
    slab_blocks, slab_rows, slab_cols = pieces
    device_parts = jax.vmap(forward)(slab_blocks, slab_rows, slab_cols, vectors)
    return lax.optimization_barrier(jnp.sum(device_parts, axis=0))

def add_backward(running, pieces):
    slab_blocks, slab_rows, slab_cols, slab_vectors = pieces
    device_parts = jax.vmap(backward, in_axes=(0, 0, 0, None))(slab_blocks, slab_rows, slab_cols, slab_vectors)
    return (running + device_parts, None)

def reference(tile_blocks, tile_row, tile_col, tile_count, column_costs, demand, primal_start, dual_start):
    grid_blocks = tile_blocks.reshape(N_ROWS, N_COLS, SLOTS, TILE, TILE)
    grid_rows = tile_row.reshape(N_ROWS, N_COLS, SLOTS)
    grid_cols = tile_col.reshape(N_ROWS, N_COLS, SLOTS)
    row_hot, col_hot = jax.vmap(jax.vmap(slot_tables))(grid_rows, grid_cols, tile_count)
    row_scale = jnp.ones((N_ROWS, ROW_BLOCKS, TILE), jnp.float32)
    col_scale = jnp.ones((N_COLS, COL_BLOCKS, TILE), jnp.float32)
    for sweep_index in range(SWEEPS):
        row_max, col_parts = lax.map(partial(slab_extremes, col_scale=col_scale), (grid_blocks, row_hot, col_hot, row_scale))
        col_max = lax.optimization_barrier(jnp.max(col_parts, axis=0))
        row_scale = row_scale / jnp.sqrt(row_max + EPSILON)
        col_scale = col_scale / jnp.sqrt(col_max + EPSILON)
    row_sum, col_parts = lax.map(partial(slab_totals, col_scale=col_scale), (grid_blocks, row_hot, col_hot, row_scale))
    col_sum = lax.optimization_barrier(jnp.sum(col_parts, axis=0))
    step_size = 0.95 / jnp.sqrt(jnp.max(row_sum) * jnp.max(col_sum))
    cost_hat = col_scale * column_costs.reshape(N_COLS, COL_BLOCKS, TILE)
    demand_hat = row_scale[..., None] * demand.astype(jnp.float32).reshape(N_ROWS, ROW_BLOCKS, TILE, SCENARIOS)
    primal = primal_start.reshape(N_COLS, COL_BLOCKS, TILE, SCENARIOS) / col_scale[..., None]
    dual_now = dual_start.reshape(N_ROWS, ROW_BLOCKS, TILE, SCENARIOS) / row_scale[..., None]
    weight = jnp.ones((SCENARIOS,), jnp.float32)
    residual = demand_hat
    for iteration in range(ITERS):
        summed = lax.scan(add_backward, jnp.zeros((N_COLS, COL_BLOCKS, TILE, SCENARIOS), jnp.float32), (grid_blocks, row_hot, col_hot, row_scale[..., None] * dual_now))[0]
        gradient = cost_hat[..., None] - col_scale[..., None] * summed
        new_primal = jnp.maximum(primal - step_size / weight * gradient, 0.0)
        extended = 2.0 * new_primal - primal
        row_image = lax.map(partial(slab_forward, vectors=col_scale[..., None] * extended), (grid_blocks, row_hot, col_hot))
        residual = demand_hat - row_scale[..., None] * row_image
        new_dual = dual_now + step_size * weight * residual
        primal_moves = lax.optimization_barrier(jnp.sum(jnp.square(new_primal - primal), axis=(0, 1, 2)))
        dual_moves = lax.optimization_barrier(jnp.sum(jnp.square(new_dual - dual_now), axis=(0, 1, 2)))
        weight = jnp.sqrt(weight * jnp.sqrt((dual_moves + EPSILON) / (primal_moves + EPSILON)))
        primal = new_primal
        dual_now = new_dual
    solution = (col_scale[..., None] * primal).reshape(PRIMALS, SCENARIOS)
    dual_values = (row_scale[..., None] * dual_now).reshape(DUALS, SCENARIOS)
    return (solution, dual_values, residual.reshape(DUALS, SCENARIOS), weight)
```

```python
import functools

import jax
import jax.numpy as jnp
from jax import lax
from jax.experimental import pallas as pl
from jax.experimental.pallas import tpu as pltpu
from jax.sharding import PartitionSpec as P

NZ, NY, NX, NK = 16, 4, 4, 2
NS = NY * NK
SCEN = 32
HALVES = 2
W = SCEN // HALVES
SR = W // 2 + W // 16
ITERS = 4
EPSILON = 1e-06
MESH = pl.DeviceIdType.MESH
F32, BF16 = jnp.float32, jnp.bfloat16


def kernel(
    row_ref, col_ref, count_ref, tiles_ref, costs_ref, demand_ref, primal_ref, dual_ref,
    sol_ref, dv_ref, res_ref, w_ref,
    la, ab, at, dd, yd, pt, px, cost, rsc, rsr, csr, part, rx, cz, g, rsb, gs, mrow, fx, xs, ydo, solt, drt, mz, wy,
    dd_s, dd_r, la_s, la_r, sb_s, sb_r, pt_s, pt_r, ct_s, ct_r, rx_s, rx_r, cz_s, cz_r,
    rs_s, rs_r, ag_s, ag_r, fx_s, fx_r, so_s, so_r, dr_s, dr_r, mz_s, mz_r, wy_s, wy_r,
):
    rows, cols = lax.axis_index("rows"), lax.axis_index("cols")
    z, y, x, k = rows // NY, rows % NY, cols // NK, cols % NK
    s = y * NK + k

    def dev(zz, yy, xx, kk):
        return (zz * NY + yy, xx * NK + kk)

    def put(src, dst, ss, rs, device):
        pltpu.make_async_remote_copy(
            src_ref=src, dst_ref=dst, send_sem=ss, recv_sem=rs, device_id=device, device_id_type=MESH
        ).start()

    def drain(ref, sem):
        pltpu.make_async_copy(ref, ref, sem).wait()

    def z_far_first(send):
        def step(i, carry):
            turn = (i + 1) // 2
            d = 8 + turn - 2 * turn * (i % 2)
            send(d, (z + d) % NZ)
            return carry

        lax.fori_loop(0, NZ - 1, step, 0)

    def scen(block):
        return pl.ds(pl.multiple_of(SCEN * block, SCEN), SCEN)

    sibling = dev(z, y, x, 1 - k)
    y_others = [(y + d) % NY for d in (1, 3, 2)]
    x_others = [(x + d) % NX for d in (2, 1, 3)]
    s_others = [(s + d) % NS for d in (4, 3, 5, 2, 6, 1, 7)]

    barrier = pltpu.get_barrier_semaphore()

    def greet(d, zz):
        pl.semaphore_signal(barrier, inc=1, device_id=dev(zz, y, x, k), device_id_type=MESH)

    z_far_first(greet)
    for xx in x_others:
        pl.semaphore_signal(barrier, inc=1, device_id=dev(z, y, xx, k), device_id_type=MESH)
    for ss in s_others:
        pl.semaphore_signal(barrier, inc=1, device_id=dev(z, ss // NK, x, ss % NK), device_id_type=MESH)

    for rb in range(2):
        for cb in range(4):
            slot = jnp.int32(0)
            for t in range(8):
                same = jnp.logical_and(row_ref[0, t] == rb, col_ref[0, t] == cb)
                slot = jnp.where(same, t, slot)
            live = slot < count_ref[0, 0]
            block = tiles_ref[slot].astype(F32)
            la[s, 128 * rb : 128 * rb + 128, 128 * cb : 128 * cb + 128] = jnp.where(live, block, 0.0)
    for a in range(2):
        dd[0, a] = dual_ref[128 * a : 128 * a + 128, :].T
        dd[1, a] = demand_ref[128 * a : 128 * a + 128, :].astype(F32).T
    for c in range(4):
        pt[c] = primal_ref[128 * c : 128 * c + 128, :].T
    cost[k, 0:4, :] = costs_ref[...]
    cost[k, 4:8, :] = jnp.zeros((4, 128), F32)
    for a in range(2):
        for kind in range(2):
            yd[kind, 2 * y + a] = dd[kind, a, scen(s), :]
    for c in range(4):
        px[4 * k + c] = pt[c, scen(s), :]

    pl.semaphore_wait(barrier, NZ - 1 + NX - 1 + NS - 1)

    put(la.at[s], la.at[s], sb_s, sb_r.at[y], sibling)
    put(
        pt.at[:, scen(2 * y + 1 - k), :], px.at[pl.ds(4 * k, 4)], pt_s, pt_r, sibling
    )
    put(cost.at[k], cost.at[k], ct_s, ct_r, sibling)
    for yy in y_others:
        put(
            dd.at[:, :, scen(yy * NK + k), :], yd.at[:, pl.ds(2 * y, 2)], dd_s, dd_r, dev(z, yy, x, k)
        )
    for yy in y_others:
        put(la.at[s], la.at[s], la_s, la_r.at[y], dev(z, yy, x, k))
    for d in (3, 1, 2):
        yy = (y + d) % NY
        block = yy * NK + k
        drain(la.at[block], la_r.at[yy])
        put(la.at[block], la.at[block], sb_s, sb_r.at[yy], sibling)
    for yy in range(NY):
        drain(la.at[yy * NK + 1 - k], sb_r.at[yy])
    drain(px.at[pl.ds(0, 4)], pt_r)
    drain(cost.at[0], ct_r)
    drain(yd.at[:, pl.ds(0, 6)], dd_r)

    def partials(op, reduce, scaled):
        def step(i, accs):
            row_acc, new = None, []
            for j in range(8):
                tile = jnp.abs(
                    la[
                        2 * (i // 2) + j // 4,
                        pl.ds(pl.multiple_of(128 * (i % 2), 128), 128),
                        128 * (j % 4) : 128 * (j % 4) + 128,
                    ]
                )
                if scaled:
                    tile = tile * rsc[i] * csr[j : j + 1, :]
                row_acc = tile if row_acc is None else op(row_acc, tile)
                new.append(op(accs[j], reduce(tile.reshape(16, 8, 128), axis=0)))
            part[0, pl.ds(i, 1), :] = reduce(row_acc.T, axis=0, keepdims=True)
            return tuple(new)

        accs = lax.fori_loop(0, 8, step, tuple(jnp.zeros((8, 128), F32) for _ in range(8)))
        for j in range(8):
            part[1, j : j + 1, :] = reduce(accs[j], axis=0, keepdims=True)

    def send_x(use, value):
        rx[use, x] = value
        for xx in x_others:
            put(rx.at[use, x], rx.at[use, x], rx_s.at[use], rx_r.at[use], dev(z, y, xx, k))

    def send_z(use, value):
        cz[use, z] = value
        z_far_first(
            lambda d, zz: put(cz.at[use, z], cz.at[use, z], cz_s.at[use], cz_r.at[use], dev(zz, y, x, k))
        )

    def wait_x(use):
        drain(rx.at[use, pl.ds(0, NX - 1)], rx_r.at[use])
        drain(rx.at[use, pl.ds(0, NX - 1)], rx_s.at[use])

    def wait_z(use):
        drain(cz.at[use, pl.ds(0, NZ - 1)], cz_r.at[use])
        drain(cz.at[use, pl.ds(0, NZ - 1)], cz_s.at[use])

    def rescale(use):
        wait_x(use)
        rsr[...] = rsr[...] / jnp.sqrt(jnp.max(rx[use], axis=0) + EPSILON)
        for i in range(8):
            rsc[i] = jnp.broadcast_to(rsr[i : i + 1, :], (128, 128)).T
        wait_z(use)
        csr[...] = csr[...] / jnp.sqrt(jnp.max(cz[use], axis=0) + EPSILON)

    def product(value, matrix):
        high = value.astype(BF16)
        low = (value - high.astype(F32)).astype(BF16)
        both = jnp.dot(jnp.concatenate([high, low], axis=0), matrix[...], preferred_element_type=F32)
        return both[:W] + both[W:]

    def backward(h, duals, moves):
        result = product(jnp.concatenate(duals, axis=1), ab)
        for j in range(8):
            for q in range(2):
                g[h, 2 * j + q, 0 : W // 2, :] = result[
                    q * (W // 2) : (q + 1) * (W // 2), 128 * j : 128 * j + 128
                ]
        n = W // 16
        for i in range(16):
            g[h, i, W // 2 : SR, :] = moves[i * n : (i + 1) * n, :]
        z_far_first(
            lambda d, zz: put(g.at[h, zz], rsb.at[h, d - 1], rs_s.at[h], rs_r.at[h], dev(zz, y, x, k))
        )

    def sum_and_spread(h):
        drain(rsb.at[h], rs_r.at[h])
        total = g[h, z]
        for d in range(NZ - 1):
            total = total + rsb[h, d]
        gs[h, z] = total
        z_far_first(
            lambda d, zz: put(gs.at[h, z], gs.at[h, z], ag_s.at[h], ag_r.at[h], dev(zz, y, x, k))
        )
        drain(rsb.at[h], rs_s.at[h])

    def part_of(h):
        return slice(h * W, (h + 1) * W)

    rsr[...] = jnp.ones((8, 128), F32)
    csr[...] = jnp.ones((8, 128), F32)
    partials(jnp.maximum, jnp.max, False)
    send_x(0, part[0])
    send_z(0, part[1])
    for b in range(8):
        ab[256 * (b // 2) : 256 * (b // 2) + 256, 512 * (b % 2) : 512 * (b % 2) + 512] = la[b].astype(BF16)
    for h in range(HALVES):
        backward(h, [yd[0, i, part_of(h), :] for i in range(8)], jnp.zeros((W, 128), F32))
    rescale(0)
    partials(jnp.maximum, jnp.max, True)
    send_x(1, part[0])
    send_z(1, part[1])
    for h in range(HALVES):
        sum_and_spread(h)
    for b in range(8):
        at[512 * (b % 2) : 512 * (b % 2) + 512, 256 * (b // 2) : 256 * (b // 2) + 256] = la[b].T.astype(BF16)
    rescale(1)
    partials(jnp.add, jnp.sum, True)
    send_x(2, part[0])
    send_z(2, part[1])
    for i in range(8):
        yd[0, i] = yd[0, i] / rsr[i : i + 1, :]
        yd[1, i] = yd[1, i] * rsr[i : i + 1, :]
        px[i] = px[i] / csr[i : i + 1, :]
    part[1] = csr[...] * jnp.concatenate([cost[0, 0:4, :], cost[1, 0:4, :]], axis=0)
    wait_x(2)
    row_sum = rx[2, 0] + rx[2, 1] + rx[2, 2] + rx[2, 3]
    send_z(3, row_sum)
    wait_z(2)
    col_sum = cz[2, 0]
    for i in range(1, NZ):
        col_sum = col_sum + cz[2, i]
    send_x(3, col_sum)
    wait_x(3)
    wait_z(3)

    def largest(tiles):
        return jnp.max(jnp.max(jnp.max(tiles, axis=0), axis=1, keepdims=True), axis=0, keepdims=True)

    step_size = 0.95 / jnp.sqrt(largest(cz[3]) * largest(rx[3]))

    weight = [jnp.ones((W, 1), F32) for _ in range(HALVES)]
    primal_moves = [None] * HALVES
    dual_moves = [None] * HALVES
    for t in range(ITERS):
        slot = t % 2
        last = t == ITERS - 1
        if t > 0:
            for h in range(HALVES):
                sum_and_spread(h)
        for h in range(HALVES):
            drain(gs.at[h, pl.ds(0, NZ - 1)], ag_r.at[h])
            if t > 0:
                n = W // 16
                for i in range(16):
                    mrow[h, i * n : (i + 1) * n, :] = gs[h, i, W // 2 : SR, :]
                moved = jnp.sum(mrow[h], axis=1, keepdims=True)
                weight[h] = jnp.sqrt(
                    weight[h] * jnp.sqrt((moved + EPSILON) / (primal_moves[h] + EPSILON))
                )
            rate = step_size / weight[h]
            moves, extended = jnp.zeros((W, 128), F32), []
            for j in range(8):
                scale = csr[j : j + 1, :]
                summed = jnp.concatenate(
                    [gs[h, 2 * j, 0 : W // 2, :], gs[h, 2 * j + 1, 0 : W // 2, :]], axis=0
                )
                old = px[j, part_of(h), :]
                new = jnp.maximum(old - rate * (part[1, j : j + 1, :] - scale * summed), 0.0)
                moves = moves + jnp.square(new - old)
                extended.append(scale * (2.0 * new - old))
                px[j, part_of(h), :] = new
                if last:
                    xs[j, part_of(h), :] = scale * new
            image = product(jnp.concatenate(extended, axis=1), at)
            for i in range(8):
                fx[slot, h, x, i] = image[:, 128 * i : 128 * i + 128]
            fx[slot, h, x, 8] = moves
            for xx in x_others:
                put(
                    fx.at[slot, h, x], fx.at[slot, h, x], fx_s.at[slot, h], fx_r.at[slot, h], dev(z, y, xx, k)
                )
            drain(gs.at[h, pl.ds(0, NZ - 1)], ag_s.at[h])
        if last:
            for c in range(4):
                solt[c, scen(s), :] = xs[4 * k + c]
            for ss in s_others:
                put(
                    xs.at[pl.ds(4 * (ss % NK), 4)], solt.at[:, scen(s), :], so_s, so_r,
                    dev(z, ss // NK, x, ss % NK),
                )
        for h in range(HALVES):
            drain(fx.at[slot, h, pl.ds(0, NX - 1)], fx_r.at[slot, h])
            rate = step_size * weight[h]
            moves, duals = jnp.zeros((W, 128), F32), []
            for i in range(8):
                scale = rsr[i : i + 1, :]
                image = fx[slot, h, 0, i] + fx[slot, h, 1, i] + fx[slot, h, 2, i] + fx[slot, h, 3, i]
                residual = yd[1, i, part_of(h), :] - scale * image
                old = yd[0, i, part_of(h), :]
                new = old + rate * residual
                moves = moves + jnp.square(new - old)
                yd[0, i, part_of(h), :] = new
                duals.append(scale * new)
                if last:
                    ydo[0, i, part_of(h), :] = scale * new
                    ydo[1, i, part_of(h), :] = residual
            primal_moves[h] = jnp.sum(
                fx[slot, h, 0, 8] + fx[slot, h, 1, 8] + fx[slot, h, 2, 8] + fx[slot, h, 3, 8],
                axis=1, keepdims=True,
            )
            if last:
                dual_moves[h] = jnp.sum(moves, axis=1, keepdims=True)
            else:
                backward(h, duals, moves)
            drain(fx.at[slot, h, pl.ds(0, NX - 1)], fx_s.at[slot, h])

    lane = lax.broadcasted_iota(jnp.int32, (8, 128), 1)

    def packed(columns):
        column = jnp.concatenate(columns, axis=0)
        tile = jnp.zeros((8, 128), F32)
        for q in range(4):
            tile = jnp.where(lane == q, column[8 * q : 8 * q + 8], tile)
        return tile

    mz[z] = packed(dual_moves)
    z_far_first(lambda d, zz: put(mz.at[z], mz.at[z], mz_s, mz_r, dev(zz, y, x, k)))
    for a in range(2):
        for kind in range(2):
            drt[kind, a, scen(s), :] = ydo[kind, 2 * y + a]
    for ss in s_others:
        put(
            ydo.at[:, pl.ds(2 * (ss // NK), 2)], drt.at[:, :, scen(s), :], dr_s, dr_r,
            dev(z, ss // NK, x, ss % NK),
        )
    drain(solt.at[:, pl.ds(0, SCEN * (NS - 1)), :], so_r)
    for c in range(4):
        sol_ref[128 * c : 128 * c + 128, :] = solt[c].T
    drain(mz.at[pl.ds(0, NZ - 1)], mz_r)
    moved = mz[0]
    for i in range(1, NZ):
        moved = moved + mz[i]
    wy[s] = jnp.sqrt(
        packed(weight) * jnp.sqrt((moved + EPSILON) / (packed(primal_moves) + EPSILON))
    )
    for ss in s_others:
        put(wy.at[s], wy.at[s], wy_s, wy_r, dev(z, ss // NK, x, ss % NK))
    drain(drt.at[:, :, pl.ds(0, SCEN * (NS - 1)), :], dr_r)
    for a in range(2):
        dv_ref[128 * a : 128 * a + 128, :] = drt[0, a].T
        res_ref[128 * a : 128 * a + 128, :] = drt[1, a].T
    drain(wy.at[pl.ds(0, NS - 1)], wy_r)
    gathered = jnp.zeros((8, 128), F32)
    for b in range(NS):
        tile = jnp.where(lane < 4, wy[b], 0.0)
        gathered = gathered + (tile if b == 0 else pltpu.roll(tile, 4 * b, 1))
    turned = jnp.concatenate([gathered, jnp.zeros((120, 128), F32)], axis=0).T[:SCEN]
    for shift in (8, 16, 32, 64):
        turned = turned + pltpu.roll(turned, shift, 1)
    group = lax.broadcasted_iota(jnp.int32, (SCEN, 128), 0)
    eighth = lax.broadcasted_iota(jnp.int32, (SCEN, 128), 1) // 8
    w_ref[0:1, :] = jnp.sum(jnp.where(group == eighth, turned, 0.0), axis=0, keepdims=True)
    w_ref[1:2, :] = jnp.sum(jnp.where(group == eighth + 16, turned, 0.0), axis=0, keepdims=True)

    drain(la.at[pl.ds(0, NY - 1)], la_s)
    drain(la.at[pl.ds(0, NY)], sb_s)
    drain(px.at[pl.ds(0, 4)], pt_s)
    drain(cost.at[0], ct_s)
    drain(yd.at[:, pl.ds(0, 6)], dd_s)
    drain(solt.at[:, pl.ds(0, SCEN * (NS - 1)), :], so_s)
    drain(mz.at[pl.ds(0, NZ - 1)], mz_s)
    drain(drt.at[:, :, pl.ds(0, SCEN * (NS - 1)), :], dr_s)
    drain(wy.at[pl.ds(0, NS - 1)], wy_s)


def body(
    tile_blocks, tile_row, tile_col, tile_count, column_costs, demand, primal_start, dual_start
):
    smem = pl.BlockSpec(memory_space=pltpu.SMEM)
    vmem = pl.BlockSpec(memory_space=pltpu.VMEM)
    dma = pltpu.SemaphoreType.DMA
    solution_, duals, residual, weight = pl.pallas_call(
        kernel,
        out_shape=(
            jax.ShapeDtypeStruct((512, 256), F32),
            jax.ShapeDtypeStruct((256, 256), F32),
            jax.ShapeDtypeStruct((256, 256), F32),
            jax.ShapeDtypeStruct((2, 128), F32),
        ),
        in_specs=[smem, smem, smem, vmem, vmem, vmem, vmem, vmem],
        out_specs=(vmem, vmem, vmem, vmem),
        scratch_shapes=[
            pltpu.VMEM((8, 256, 512), F32),
            pltpu.VMEM((1024, 1024), BF16),
            pltpu.VMEM((1024, 1024), BF16),
            pltpu.VMEM((2, 2, 256, 128), F32),
            pltpu.VMEM((2, 8, SCEN, 128), F32),
            pltpu.VMEM((4, 256, 128), F32),
            pltpu.VMEM((8, SCEN, 128), F32),
            pltpu.VMEM((2, 8, 128), F32),
            pltpu.VMEM((8, 128, 128), F32),
            pltpu.VMEM((8, 128), F32),
            pltpu.VMEM((8, 128), F32),
            pltpu.VMEM((2, 8, 128), F32),
            pltpu.VMEM((4, NX, 8, 128), F32),
            pltpu.VMEM((4, NZ, 8, 128), F32),
            pltpu.VMEM((HALVES, NZ, SR, 128), F32),
            pltpu.VMEM((HALVES, NZ - 1, SR, 128), F32),
            pltpu.VMEM((HALVES, NZ, SR, 128), F32),
            pltpu.VMEM((HALVES, W, 128), F32),
            pltpu.VMEM((2, HALVES, NX, 9, W, 128), F32),
            pltpu.VMEM((8, SCEN, 128), F32),
            pltpu.VMEM((2, 8, SCEN, 128), F32),
            pltpu.VMEM((4, 256, 128), F32),
            pltpu.VMEM((2, 2, 256, 128), F32),
            pltpu.VMEM((NZ, 8, 128), F32),
            pltpu.VMEM((NS, 8, 128), F32),
            dma, dma,
            dma, dma((NY,)),
            dma, dma((NY,)),
            dma, dma,
            dma, dma,
            dma((4,)), dma((4,)),
            dma((4,)), dma((4,)),
            dma((HALVES,)), dma((HALVES,)),
            dma((HALVES,)), dma((HALVES,)),
            dma((2, HALVES)), dma((2, HALVES)),
            dma, dma,
            dma, dma,
            dma, dma,
            dma, dma,
        ],
        compiler_params=pltpu.CompilerParams(
            collective_id=0, has_side_effects=True, vmem_limit_bytes=40 << 20
        ),
    )(
        tile_row, tile_col, tile_count, tile_blocks[0], column_costs.reshape(4, 128), demand, primal_start, dual_start
    )
    return solution_, duals, residual, weight.reshape(256)


def solution(mesh):
    return jax.shard_map(
        body,
        mesh=mesh,
        in_specs=(
            P("rows", "cols", None, None),
            P("rows", "cols"),
            P("rows", "cols"),
            P("rows", "cols"),
            P("cols"),
            P("rows", None),
            P("cols", None),
            P("rows", None),
        ),
        out_specs=(P("cols", None), P("rows", None), P("rows", None), P()),
        check_vma=False,
    )
```

```python
import functools

import jax
import jax.numpy as jnp
from jax import lax
from jax.experimental import pallas as pl
from jax.experimental.pallas import tpu as pltpu
from jax.sharding import PartitionSpec as P

NZ, NY, NX, NK = 16, 4, 4, 2
NS = NY * NK
PLANE = NX * NY * NK
SCEN = 32
HALVES = 2
W = SCEN // HALVES
SR = W // 2 + W // 16
ITERS = 4
EPSILON = 1e-06
MESH = pl.DeviceIdType.MESH
F32, BF16 = jnp.float32, jnp.bfloat16


def kernel(
    row_ref, col_ref, count_ref, tiles_hbm, costs_hbm, demand_hbm, primal_hbm, dual_hbm,
    sol_hbm, dv_hbm, res_hbm, w_ref,
    tiles_ref, costs_ref, demand_ref, primal_ref, dual_ref, in_s, sol_ref, dv_ref, res_ref, out_s, la, ab, at, dd, yd, pt, px, cost, rsc, rsr, csr, part, rp, cy, cz4, rx, cz, g, rsb, gs, mrow, fx, xs, ydo, solt, drt, mz, wy,
    dd_s, dd_r, la_s, la_r, sb_s, sb_r, pt_s, pt_r, ct_s, ct_r, rp_s, rp_r, cy_s, cy_r, c4_s, c4_r, rx_s, rx_r, cz_s, cz_r,
    rs_s, rs_r, ag_s, ag_r, fx_s, fx_r, so_s, so_r, dr_s, dr_r, mz_s, mz_r, wy_s, wy_r,
):
    rows, cols = lax.axis_index("rows"), lax.axis_index("cols")
    z, y, x, k = rows // NY, rows % NY, cols // NK, cols % NK
    s = y * NK + k

    def dev(zz, yy, xx, kk):
        return (zz * NY + yy, xx * NK + kk)

    def put(src, dst, ss, rs, device):
        pltpu.make_async_remote_copy(
            src_ref=src, dst_ref=dst, send_sem=ss, recv_sem=rs, device_id=device, device_id_type=MESH
        ).start()

    def drain(ref, sem):
        pltpu.make_async_copy(ref, ref, sem).wait()

    def z_far_first(send):
        def step(i, carry):
            turn = (i + 1) // 2
            d = 8 + turn - 2 * turn * (i % 2)
            send(d, (z + d) % NZ)
            return carry

        lax.fori_loop(0, NZ - 1, step, 0)

    def scen(block):
        return pl.ds(pl.multiple_of(SCEN * block, SCEN), SCEN)

    sibling = dev(z, y, x, 1 - k)
    y_others = [(y + d) % NY for d in (1, 3, 2)]
    x_others = [(x + d) % NX for d in (2, 1, 3)]
    s_others = [(s + d) % NS for d in (4, 3, 5, 2, 6, 1, 7)]

    me = y * NX * NK + cols

    def plane(send):
        def step(d, carry):
            other = (me + d) % PLANE
            send((z * NY + other // (NX * NK), other % (NX * NK)))
            return carry

        lax.fori_loop(1, PLANE, step, 0)

    barrier = pltpu.get_barrier_semaphore()

    def greet(device):
        pl.semaphore_signal(barrier, inc=1, device_id=device, device_id_type=MESH)

    z_far_first(lambda d, zz: greet(dev(zz, y, x, k)))
    plane(greet)
    inputs = [
        pltpu.make_async_copy(source, target, in_s.at[i])
        for i, (source, target) in enumerate((
            (tiles_hbm.at[0], tiles_ref), (dual_hbm, dual_ref), (demand_hbm, demand_ref),
            (primal_hbm, primal_ref), (costs_hbm, costs_ref),
        ))
    ]
    for copy in inputs:
        copy.start()

    inputs[0].wait()
    for rb in range(2):
        for cb in range(4):
            slot = jnp.int32(0)
            for t in range(8):
                same = jnp.logical_and(row_ref[0, t] == rb, col_ref[0, t] == cb)
                slot = jnp.where(same, t, slot)
            live = slot < count_ref[0, 0]
            block = tiles_ref[slot].astype(F32)
            la[s, 128 * rb : 128 * rb + 128, 128 * cb : 128 * cb + 128] = jnp.where(live, block, 0.0)
    rsr[...] = jnp.ones((8, 128), F32)
    csr[...] = jnp.ones((8, 128), F32)

    def own_partials(scaled):
        col_acc = [None] * 4
        for a in range(2):
            row_acc = None
            if scaled:
                row_scale = jnp.broadcast_to(rsr[pl.ds(2 * y + a, 1), :], (128, 128)).T
            for c in range(4):
                tile = jnp.abs(la[s, 128 * a : 128 * a + 128, 128 * c : 128 * c + 128])
                if scaled:
                    tile = tile * row_scale * csr[pl.ds(4 * k + c, 1), :]
                row_acc = tile if c == 0 else jnp.maximum(row_acc, tile)
                top = jnp.max(tile.reshape(16, 8, 128), axis=0)
                col_acc[c] = top if a == 0 else jnp.maximum(col_acc[c], top)
            part[0, a : a + 1, :] = jnp.max(row_acc.T, axis=0, keepdims=True)
        for c in range(4):
            part[1, c : c + 1, :] = jnp.max(col_acc[c], axis=0, keepdims=True)

    def send_plane(use):
        slot = cols * NY + y
        rp[use, slot] = part[0, 0:2, :]
        plane(lambda device: put(rp.at[use, slot], rp.at[use, slot], rp_s.at[use], rp_r.at[use], device))

    def rescale_rows(use):
        drain(rp.at[use, pl.ds(0, PLANE - 1)], rp_r.at[use])
        for yy in range(NY):
            top = rp[use, yy]
            for cc in range(1, NX * NK):
                top = jnp.maximum(top, rp[use, cc * NY + yy])
            both = slice(2 * yy, 2 * yy + 2)
            rsr[both, :] = rsr[both, :] / jnp.sqrt(top + EPSILON)
        drain(rp.at[use, pl.ds(0, PLANE - 1)], rp_s.at[use])

    def send_yk(use, value):
        cy[use, s] = value
        for ss in s_others:
            put(cy.at[use, s], cy.at[use, s], cy_s.at[use], cy_r.at[use], dev(z, ss // NK, x, ss % NK))

    def wait_yk(use):
        drain(cy.at[use, pl.ds(0, NS - 1)], cy_r.at[use])
        drain(cy.at[use, pl.ds(0, NS - 1)], cy_s.at[use])
        tops = []
        for kk in range(NK):
            top = cy[use, kk]
            for yy in range(1, NY):
                top = jnp.maximum(top, cy[use, yy * NK + kk])
            tops.append(top)
        return jnp.concatenate(tops, axis=0)

    own_partials(False)
    inputs[1].wait()
    inputs[2].wait()
    for a in range(2):
        dd[0, a] = dual_ref[128 * a : 128 * a + 128, :].T
        dd[1, a] = demand_ref[128 * a : 128 * a + 128, :].astype(F32).T
    inputs[3].wait()
    for c in range(4):
        pt[c] = primal_ref[128 * c : 128 * c + 128, :].T
    inputs[4].wait()
    for c in range(4):
        cost[k, c : c + 1, :] = costs_ref[128 * c : 128 * c + 128].reshape(1, 128)
    cost[k, 4:8, :] = jnp.zeros((4, 128), F32)
    for a in range(2):
        for kind in range(2):
            yd[kind, 2 * y + a] = dd[kind, a, scen(s), :]
    for c in range(4):
        px[4 * k + c] = pt[c, scen(s), :]

    pl.semaphore_wait(barrier, NZ - 1 + PLANE - 1)

    send_yk(0, part[1, 0:4, :])
    send_plane(0)

    put(la.at[s], la.at[s], sb_s, sb_r.at[y], sibling)
    put(
        pt.at[:, scen(2 * y + 1 - k), :], px.at[pl.ds(4 * k, 4)], pt_s, pt_r, sibling
    )
    put(cost.at[k], cost.at[k], ct_s, ct_r, sibling)
    for yy in y_others:
        put(
            dd.at[:, :, scen(yy * NK + k), :], yd.at[:, pl.ds(2 * y, 2)], dd_s, dd_r, dev(z, yy, x, k)
        )
    up, down = (y + 1) % NY, (y + 3) % NY

    def half(yy, n):
        return la.at[yy * NK + k, 128 * n : 128 * n + 128]

    def pass_on(yy, n, to):
        put(half(yy, n), half(yy, n), la_s, la_r.at[n, yy], dev(z, to, x, k))

    def arrived(yy, n):
        drain(half(yy, n), la_r.at[n, yy])
        put(half(yy, n), half(yy, n), sb_s, sb_r.at[yy], sibling)

    pass_on(y, 0, up)
    pass_on(y, 1, down)
    pass_on(y, 1, up)
    pass_on(y, 0, down)
    def partials(op, reduce, scaled):
        def step(i, accs):
            row_acc, new = None, []
            for j in range(8):
                tile = jnp.abs(
                    la[
                        2 * (i // 2) + j // 4,
                        pl.ds(pl.multiple_of(128 * (i % 2), 128), 128),
                        128 * (j % 4) : 128 * (j % 4) + 128,
                    ]
                )
                if scaled:
                    tile = tile * rsc[i] * csr[j : j + 1, :]
                row_acc = tile if row_acc is None else op(row_acc, tile)
                new.append(op(accs[j], reduce(tile.reshape(16, 8, 128), axis=0)))
            part[0, pl.ds(i, 1), :] = reduce(row_acc.T, axis=0, keepdims=True)
            return tuple(new)

        accs = lax.fori_loop(0, 8, step, tuple(jnp.zeros((8, 128), F32) for _ in range(8)))
        for j in range(8):
            part[1, j : j + 1, :] = reduce(accs[j], axis=0, keepdims=True)

    def send_x(use, value):
        rx[use, x] = value
        for xx in x_others:
            put(rx.at[use, x], rx.at[use, x], rx_s.at[use], rx_r.at[use], dev(z, y, xx, k))

    def send_z(use, value):
        cz[use, z] = value
        z_far_first(
            lambda d, zz: put(cz.at[use, z], cz.at[use, z], cz_s.at[use], cz_r.at[use], dev(zz, y, x, k))
        )

    def wait_x(use):
        drain(rx.at[use, pl.ds(0, NX - 1)], rx_r.at[use])
        drain(rx.at[use, pl.ds(0, NX - 1)], rx_s.at[use])

    def wait_z(use):
        drain(cz.at[use, pl.ds(0, NZ - 1)], cz_r.at[use])
        drain(cz.at[use, pl.ds(0, NZ - 1)], cz_s.at[use])

    def product(value, matrix):
        high = value.astype(BF16)
        low = (value - high.astype(F32)).astype(BF16)
        both = jnp.dot(jnp.concatenate([high, low], axis=0), matrix[...], preferred_element_type=F32)
        return both[:W] + both[W:]

    def backward(h, duals, moves):
        result = product(jnp.concatenate(duals, axis=1), ab)
        for j in range(8):
            for q in range(2):
                g[h, 2 * j + q, 0 : W // 2, :] = result[
                    q * (W // 2) : (q + 1) * (W // 2), 128 * j : 128 * j + 128
                ]
        n = W // 16
        for i in range(16):
            g[h, i, W // 2 : SR, :] = moves[i * n : (i + 1) * n, :]
        z_far_first(
            lambda d, zz: put(g.at[h, zz], rsb.at[h, d - 1], rs_s.at[h], rs_r.at[h], dev(zz, y, x, k))
        )

    def sum_and_spread(h):
        drain(rsb.at[h], rs_r.at[h])
        total = g[h, z]
        for d in range(NZ - 1):
            total = total + rsb[h, d]
        gs[h, z] = total
        z_far_first(
            lambda d, zz: put(gs.at[h, z], gs.at[h, z], ag_s.at[h], ag_r.at[h], dev(zz, y, x, k))
        )
        drain(rsb.at[h], rs_s.at[h])

    def part_of(h):
        return slice(h * W, (h + 1) * W)

    send_z(0, wait_yk(0))
    rescale_rows(0)
    arrived(down, 0)
    pass_on(down, 0, up)
    arrived(up, 1)
    pass_on(up, 1, down)
    wait_z(0)
    csr[...] = csr[...] / jnp.sqrt(jnp.max(cz[0], axis=0) + EPSILON)
    own_partials(True)
    cz4[z] = part[1, 0:4, :]
    z_far_first(lambda d, zz: put(cz4.at[z], cz4.at[z], c4_s, c4_r, dev(zz, y, x, k)))
    send_plane(1)
    arrived(up, 0)
    arrived(down, 1)
    arrived((y + 2) % NY, 0)
    arrived((y + 2) % NY, 1)
    rescale_rows(1)
    drain(cz4.at[pl.ds(0, NZ - 1)], c4_r)
    drain(cz4.at[pl.ds(0, NZ - 1)], c4_s)
    send_yk(1, jnp.max(cz4[...], axis=0))
    for yy in range(NY):
        drain(la.at[yy * NK + 1 - k], sb_r.at[yy])
    drain(yd.at[:, pl.ds(0, 6)], dd_r)
    for b in range(8):
        ab[256 * (b // 2) : 256 * (b // 2) + 256, 512 * (b % 2) : 512 * (b % 2) + 512] = la[b].astype(BF16)
    for i in range(8):
        rsc[i] = jnp.broadcast_to(rsr[i : i + 1, :], (128, 128)).T
    for h in range(HALVES):
        backward(h, [yd[0, i, part_of(h), :] for i in range(8)], jnp.zeros((W, 128), F32))
    csr[...] = csr[...] / jnp.sqrt(wait_yk(1) + EPSILON)
    partials(jnp.add, jnp.sum, True)
    send_x(0, part[0])
    send_z(1, part[1])
    wait_x(0)
    send_z(2, rx[0, 0] + rx[0, 1] + rx[0, 2] + rx[0, 3])
    for h in range(HALVES):
        sum_and_spread(h)
    for b in range(8):
        at[512 * (b % 2) : 512 * (b % 2) + 512, 256 * (b // 2) : 256 * (b // 2) + 256] = la[b].T.astype(BF16)
    wait_z(1)
    col_sum = cz[1, 0]
    for i in range(1, NZ):
        col_sum = col_sum + cz[1, i]
    send_x(1, col_sum)
    drain(px.at[pl.ds(0, 4)], pt_r)
    drain(cost.at[0], ct_r)
    for i in range(8):
        yd[0, i] = yd[0, i] / rsr[i : i + 1, :]
        yd[1, i] = yd[1, i] * rsr[i : i + 1, :]
        px[i] = px[i] / csr[i : i + 1, :]
    part[1] = csr[...] * jnp.concatenate([cost[0, 0:4, :], cost[1, 0:4, :]], axis=0)
    wait_x(1)
    wait_z(2)

    def largest(tiles):
        return jnp.max(jnp.max(jnp.max(tiles, axis=0), axis=1, keepdims=True), axis=0, keepdims=True)

    step_size = 0.95 / jnp.sqrt(largest(cz[2]) * largest(rx[1]))

    weight = [jnp.ones((W, 1), F32) for _ in range(HALVES)]
    primal_moves = [None] * HALVES
    dual_moves = [None] * HALVES
    for t in range(ITERS):
        slot = t % 2
        last = t == ITERS - 1
        if t > 0:
            for h in range(HALVES):
                sum_and_spread(h)
        for h in range(HALVES):
            drain(gs.at[h, pl.ds(0, NZ - 1)], ag_r.at[h])
            if t > 0:
                n = W // 16
                for i in range(16):
                    mrow[h, i * n : (i + 1) * n, :] = gs[h, i, W // 2 : SR, :]
                moved = jnp.sum(mrow[h], axis=1, keepdims=True)
                weight[h] = jnp.sqrt(
                    weight[h] * jnp.sqrt((moved + EPSILON) / (primal_moves[h] + EPSILON))
                )
            rate = step_size / weight[h]
            moves, extended = jnp.zeros((W, 128), F32), []
            for j in range(8):
                scale = csr[j : j + 1, :]
                summed = jnp.concatenate(
                    [gs[h, 2 * j, 0 : W // 2, :], gs[h, 2 * j + 1, 0 : W // 2, :]], axis=0
                )
                old = px[j, part_of(h), :]
                new = jnp.maximum(old - rate * (part[1, j : j + 1, :] - scale * summed), 0.0)
                moves = moves + jnp.square(new - old)
                extended.append(scale * (2.0 * new - old))
                px[j, part_of(h), :] = new
                if last:
                    xs[j, part_of(h), :] = scale * new
            image = product(jnp.concatenate(extended, axis=1), at)
            for i in range(8):
                fx[slot, h, x, i] = image[:, 128 * i : 128 * i + 128]
            fx[slot, h, x, 8] = moves
            for xx in x_others:
                put(
                    fx.at[slot, h, x], fx.at[slot, h, x], fx_s.at[slot, h], fx_r.at[slot, h], dev(z, y, xx, k)
                )
            drain(gs.at[h, pl.ds(0, NZ - 1)], ag_s.at[h])
        if last:
            for c in range(4):
                solt[c, scen(s), :] = xs[4 * k + c]
            for ss in s_others:
                put(
                    xs.at[pl.ds(4 * (ss % NK), 4)], solt.at[:, scen(s), :], so_s, so_r,
                    dev(z, ss // NK, x, ss % NK),
                )
        for h in range(HALVES):
            drain(fx.at[slot, h, pl.ds(0, NX - 1)], fx_r.at[slot, h])
            rate = step_size * weight[h]
            moves, duals = jnp.zeros((W, 128), F32), []
            for i in range(8):
                scale = rsr[i : i + 1, :]
                image = fx[slot, h, 0, i] + fx[slot, h, 1, i] + fx[slot, h, 2, i] + fx[slot, h, 3, i]
                residual = yd[1, i, part_of(h), :] - scale * image
                old = yd[0, i, part_of(h), :]
                new = old + rate * residual
                moves = moves + jnp.square(new - old)
                yd[0, i, part_of(h), :] = new
                duals.append(scale * new)
                if last:
                    ydo[0, i, part_of(h), :] = scale * new
                    ydo[1, i, part_of(h), :] = residual
            primal_moves[h] = jnp.sum(
                fx[slot, h, 0, 8] + fx[slot, h, 1, 8] + fx[slot, h, 2, 8] + fx[slot, h, 3, 8],
                axis=1, keepdims=True,
            )
            if last:
                dual_moves[h] = jnp.sum(moves, axis=1, keepdims=True)
            else:
                backward(h, duals, moves)
            drain(fx.at[slot, h, pl.ds(0, NX - 1)], fx_s.at[slot, h])

    lane = lax.broadcasted_iota(jnp.int32, (8, 128), 1)

    def packed(columns):
        column = jnp.concatenate(columns, axis=0)
        tile = jnp.zeros((8, 128), F32)
        for q in range(4):
            tile = jnp.where(lane == q, column[8 * q : 8 * q + 8], tile)
        return tile

    mz[z] = packed(dual_moves)
    z_far_first(lambda d, zz: put(mz.at[z], mz.at[z], mz_s, mz_r, dev(zz, y, x, k)))
    for a in range(2):
        for kind in range(2):
            drt[kind, a, scen(s), :] = ydo[kind, 2 * y + a]
    for ss in s_others:
        put(
            ydo.at[:, pl.ds(2 * (ss // NK), 2)], drt.at[:, :, scen(s), :], dr_s, dr_r,
            dev(z, ss // NK, x, ss % NK),
        )
    drain(solt.at[:, pl.ds(0, SCEN * (NS - 1)), :], so_r)
    for c in range(4):
        sol_ref[128 * c : 128 * c + 128, :] = solt[c].T
    outputs = [
        pltpu.make_async_copy(sol_ref, sol_hbm, out_s.at[0]),
        pltpu.make_async_copy(dv_ref, dv_hbm, out_s.at[1]),
        pltpu.make_async_copy(res_ref, res_hbm, out_s.at[2]),
    ]
    outputs[0].start()
    drain(mz.at[pl.ds(0, NZ - 1)], mz_r)
    moved = mz[0]
    for i in range(1, NZ):
        moved = moved + mz[i]
    wy[s] = jnp.sqrt(
        packed(weight) * jnp.sqrt((moved + EPSILON) / (packed(primal_moves) + EPSILON))
    )
    for ss in s_others:
        put(wy.at[s], wy.at[s], wy_s, wy_r, dev(z, ss // NK, x, ss % NK))
    drain(drt.at[:, :, pl.ds(0, SCEN * (NS - 1)), :], dr_r)
    for a in range(2):
        dv_ref[128 * a : 128 * a + 128, :] = drt[0, a].T
        res_ref[128 * a : 128 * a + 128, :] = drt[1, a].T
    outputs[1].start()
    outputs[2].start()
    drain(wy.at[pl.ds(0, NS - 1)], wy_r)
    gathered = jnp.zeros((8, 128), F32)
    for b in range(NS):
        tile = jnp.where(lane < 4, wy[b], 0.0)
        gathered = gathered + (tile if b == 0 else pltpu.roll(tile, 4 * b, 1))
    turned = jnp.concatenate([gathered, jnp.zeros((120, 128), F32)], axis=0).T[:SCEN]
    for shift in (8, 16, 32, 64):
        turned = turned + pltpu.roll(turned, shift, 1)
    group = lax.broadcasted_iota(jnp.int32, (SCEN, 128), 0)
    eighth = lax.broadcasted_iota(jnp.int32, (SCEN, 128), 1) // 8
    w_ref[0:128] = jnp.sum(jnp.where(group == eighth, turned, 0.0), axis=0)
    w_ref[128:256] = jnp.sum(jnp.where(group == eighth + 16, turned, 0.0), axis=0)
    for copy in outputs:
        copy.wait()

    drain(la.at[pl.ds(0, NY - 1)], la_s)
    drain(la.at[pl.ds(0, NY)], sb_s)
    drain(px.at[pl.ds(0, 4)], pt_s)
    drain(cost.at[0], ct_s)
    drain(yd.at[:, pl.ds(0, 6)], dd_s)
    drain(solt.at[:, pl.ds(0, SCEN * (NS - 1)), :], so_s)
    drain(mz.at[pl.ds(0, NZ - 1)], mz_s)
    drain(drt.at[:, :, pl.ds(0, SCEN * (NS - 1)), :], dr_s)
    drain(wy.at[pl.ds(0, NS - 1)], wy_s)


def hand_over(*refs):
    sources, targets, held, sems = refs[:4], refs[4:8], refs[8:12], refs[12]
    first = [pltpu.make_async_copy(sources[i], held[i], sems.at[0, i]) for i in range(4)]
    second = [pltpu.make_async_copy(held[i], targets[i], sems.at[1, i]) for i in range(4)]
    for copy in first:
        copy.start()
    for i in (3, 1, 2, 0):
        first[i].wait()
        second[i].start()
    for copy in second:
        copy.wait()


def body(
    tile_blocks, tile_row, tile_col, tile_count, column_costs, demand, primal_start, dual_start
):
    smem = pl.BlockSpec(memory_space=pltpu.SMEM)
    vmem = pl.BlockSpec(memory_space=pltpu.VMEM)
    hbm = pl.BlockSpec(memory_space=pltpu.HBM)
    dma = pltpu.SemaphoreType.DMA
    results = pl.pallas_call(
        kernel,
        out_shape=(
            jax.ShapeDtypeStruct((512, 256), F32),
            jax.ShapeDtypeStruct((256, 256), F32),
            jax.ShapeDtypeStruct((256, 256), F32),
            jax.ShapeDtypeStruct((SCEN * NS,), F32),
        ),
        in_specs=[smem, smem, smem, hbm, hbm, hbm, hbm, hbm],
        out_specs=(hbm, hbm, hbm, vmem),
        scratch_shapes=[
            pltpu.VMEM((8, 128, 128), BF16),
            pltpu.VMEM((512,), F32),
            pltpu.VMEM((256, 256), jnp.int32),
            pltpu.VMEM((512, 256), F32),
            pltpu.VMEM((256, 256), F32),
            dma((5,)),
            pltpu.VMEM((512, 256), F32),
            pltpu.VMEM((256, 256), F32),
            pltpu.VMEM((256, 256), F32),
            dma((3,)),
            pltpu.VMEM((8, 256, 512), F32),
            pltpu.VMEM((1024, 1024), BF16),
            pltpu.VMEM((1024, 1024), BF16),
            pltpu.VMEM((2, 2, 256, 128), F32),
            pltpu.VMEM((2, 8, SCEN, 128), F32),
            pltpu.VMEM((4, 256, 128), F32),
            pltpu.VMEM((8, SCEN, 128), F32),
            pltpu.VMEM((2, 8, 128), F32),
            pltpu.VMEM((8, 128, 128), F32),
            pltpu.VMEM((8, 128), F32),
            pltpu.VMEM((8, 128), F32),
            pltpu.VMEM((2, 8, 128), F32),
            pltpu.VMEM((2, PLANE, 2, 128), F32),
            pltpu.VMEM((2, NS, 4, 128), F32),
            pltpu.VMEM((NZ, 4, 128), F32),
            pltpu.VMEM((2, NX, 8, 128), F32),
            pltpu.VMEM((3, NZ, 8, 128), F32),
            pltpu.VMEM((HALVES, NZ, SR, 128), F32),
            pltpu.VMEM((HALVES, NZ - 1, SR, 128), F32),
            pltpu.VMEM((HALVES, NZ, SR, 128), F32),
            pltpu.VMEM((HALVES, W, 128), F32),
            pltpu.VMEM((2, HALVES, NX, 9, W, 128), F32),
            pltpu.VMEM((8, SCEN, 128), F32),
            pltpu.VMEM((2, 8, SCEN, 128), F32),
            pltpu.VMEM((4, 256, 128), F32),
            pltpu.VMEM((2, 2, 256, 128), F32),
            pltpu.VMEM((NZ, 8, 128), F32),
            pltpu.VMEM((NS, 8, 128), F32),
            dma, dma,
            dma, dma((2, NY)),
            dma, dma((NY,)),
            dma, dma,
            dma, dma,
            dma((2,)), dma((2,)),
            dma((2,)), dma((2,)),
            dma, dma,
            dma((2,)), dma((2,)),
            dma((3,)), dma((3,)),
            dma((HALVES,)), dma((HALVES,)),
            dma((HALVES,)), dma((HALVES,)),
            dma((2, HALVES)), dma((2, HALVES)),
            dma, dma,
            dma, dma,
            dma, dma,
            dma, dma,
        ],
        compiler_params=pltpu.CompilerParams(
            collective_id=0, has_side_effects=True, vmem_limit_bytes=60 << 20
        ),
    )(
        tile_row, tile_col, tile_count, tile_blocks, column_costs, demand, primal_start, dual_start
    )
    return pl.pallas_call(
        hand_over,
        out_shape=tuple(jax.ShapeDtypeStruct(r.shape, F32) for r in results),
        in_specs=[hbm] * 4,
        out_specs=(hbm,) * 4,
        scratch_shapes=[pltpu.VMEM(r.shape, F32) for r in results] + [dma((2, 4))],
        compiler_params=pltpu.CompilerParams(vmem_limit_bytes=60 << 20),
    )(*results)


def solution(mesh):
    return jax.shard_map(
        body,
        mesh=mesh,
        in_specs=(
            P("rows", "cols", None, None),
            P("rows", "cols"),
            P("rows", "cols"),
            P("rows", "cols"),
            P("cols"),
            P("rows", None),
            P("cols", None),
            P("rows", None),
        ),
        out_specs=(P("cols", None), P("rows", None), P("rows", None), P()),
        check_vma=False,
    )
```

```python
import functools

import jax
import jax.numpy as jnp
from jax import lax
from jax.experimental import pallas as pl
from jax.experimental.pallas import tpu as pltpu
from jax.sharding import PartitionSpec as P

NZ, NY, NX, NK = 16, 4, 4, 2
NS = NY * NK
PLANE = NX * NY * NK
SCEN = 32
HALVES = 2
W = SCEN // HALVES
SR = W // 2 + W // 16
ITERS = 4
EPSILON = 1e-06
MESH = pl.DeviceIdType.MESH
F32, BF16 = jnp.float32, jnp.bfloat16


def kernel(
    row_ref, col_ref, count_ref, tiles_hbm, costs_hbm, demand_hbm, primal_hbm, dual_hbm,
    sol_hbm, dv_hbm, res_hbm, w_ref,
    tiles_ref, costs_ref, demand_ref, primal_ref, dual_ref, in_s, sol_ref, dv_ref, res_ref, out_s, la, ab, at, dd, yd, pt, px, cost, rsr, csr, part, bp, bq, rp, cp, cy, cz4, cz, tz, g, rsb, gs, mrow, fx, xs, ydo, solt, drt, mz, wy,
    dd_s, dd_r, la_s, la_r, sb_s, sb_r, pt_s, pt_r, ct_s, ct_r, bp_s, bp_r, rp_s, rp_r, cp_s, cp_r, cy_s, cy_r, c4_s, c4_r, cz_s, cz_r, tz_s, tz_r,
    rs_s, rs_r, ag_s, ag_r, fx_s, fx_r, so_s, so_r, dr_s, dr_r, mz_s, mz_r, wy_s, wy_r,
):
    rows, cols = lax.axis_index("rows"), lax.axis_index("cols")
    z, y, x, k = rows // NY, rows % NY, cols // NK, cols % NK
    s = y * NK + k

    def dev(zz, yy, xx, kk):
        return (zz * NY + yy, xx * NK + kk)

    def put(src, dst, ss, rs, device):
        pltpu.make_async_remote_copy(
            src_ref=src, dst_ref=dst, send_sem=ss, recv_sem=rs, device_id=device, device_id_type=MESH
        ).start()

    def drain(ref, sem):
        pltpu.make_async_copy(ref, ref, sem).wait()

    def z_far_first(send):
        def step(i, carry):
            turn = (i + 1) // 2
            d = 8 + turn - 2 * turn * (i % 2)
            send(d, (z + d) % NZ)
            return carry

        lax.fori_loop(0, NZ - 1, step, 0)

    def scen(block):
        return pl.ds(pl.multiple_of(SCEN * block, SCEN), SCEN)

    sibling = dev(z, y, x, 1 - k)
    y_others = [(y + d) % NY for d in (1, 3, 2)]
    x_others = [(x + d) % NX for d in (2, 1, 3)]
    s_others = [(s + d) % NS for d in (4, 3, 5, 2, 6, 1, 7)]

    me = y * NX * NK + cols

    def plane(send):
        def step(d, carry):
            other = (me + d) % PLANE
            send((z * NY + other // (NX * NK), other % (NX * NK)))
            return carry

        lax.fori_loop(1, PLANE, step, 0)

    barrier = pltpu.get_barrier_semaphore()

    def greet(device):
        pl.semaphore_signal(barrier, inc=1, device_id=device, device_id_type=MESH)

    z_far_first(lambda d, zz: greet(dev(zz, y, x, k)))
    plane(greet)
    inputs = [
        pltpu.make_async_copy(source, target, in_s.at[i])
        for i, (source, target) in enumerate((
            (tiles_hbm.at[0], tiles_ref), (dual_hbm, dual_ref), (demand_hbm, demand_ref),
            (primal_hbm, primal_ref), (costs_hbm, costs_ref),
        ))
    ]
    for copy in inputs:
        copy.start()

    inputs[0].wait()
    for rb in range(2):
        for cb in range(4):
            slot = jnp.int32(0)
            for t in range(8):
                same = jnp.logical_and(row_ref[0, t] == rb, col_ref[0, t] == cb)
                slot = jnp.where(same, t, slot)
            live = slot < count_ref[0, 0]
            block = tiles_ref[slot].astype(F32)
            la[s, 128 * rb : 128 * rb + 128, 128 * cb : 128 * cb + 128] = jnp.where(live, block, 0.0)
    rsr[...] = jnp.ones((8, 128), F32)
    csr[...] = jnp.ones((8, 128), F32)

    def own_partials(op, reduce, scaled):
        col_acc = [None] * 4
        for a in range(2):
            row_acc = None
            if scaled:
                row_scale = jnp.broadcast_to(rsr[pl.ds(2 * y + a, 1), :], (128, 128)).T
            for c in range(4):
                tile = jnp.abs(la[s, 128 * a : 128 * a + 128, 128 * c : 128 * c + 128])
                if scaled:
                    tile = tile * row_scale * csr[pl.ds(4 * k + c, 1), :]
                row_acc = tile if c == 0 else op(row_acc, tile)
                top = reduce(tile.reshape(16, 8, 128), axis=0)
                col_acc[c] = top if a == 0 else op(col_acc[c], top)
            part[0, a : a + 1, :] = reduce(row_acc.T, axis=0, keepdims=True)
        for c in range(4):
            part[1, c : c + 1, :] = reduce(col_acc[c], axis=0, keepdims=True)

    slot_here = cols * NY + y

    def send_plane(use):
        rp[use, slot_here] = part[0, 0:2, :]
        here = rp.at[use, slot_here]
        plane(lambda device: put(here, here, rp_s.at[use], rp_r.at[use], device))

    def send_cols(use):
        cz4[use, z] = part[1, 0:4, :]
        here = cz4.at[use, z]
        z_far_first(lambda d, zz: put(here, here, c4_s.at[use], c4_r.at[use], dev(zz, y, x, k)))

    def wait_cols(use):
        drain(cz4.at[use, pl.ds(0, NZ - 1)], c4_r.at[use])
        drain(cz4.at[use, pl.ds(0, NZ - 1)], c4_s.at[use])

    def rescale_rows(use):
        drain(rp.at[use, pl.ds(0, PLANE - 1)], rp_r.at[use])
        for yy in range(NY):
            top = rp[use, yy]
            for cc in range(1, NX * NK):
                top = jnp.maximum(top, rp[use, cc * NY + yy])
            both = slice(2 * yy, 2 * yy + 2)
            rsr[both, :] = rsr[both, :] / jnp.sqrt(top + EPSILON)
        drain(rp.at[use, pl.ds(0, PLANE - 1)], rp_s.at[use])

    def send_yk(use, value):
        cy[use, s] = value
        for ss in s_others:
            put(cy.at[use, s], cy.at[use, s], cy_s.at[use], cy_r.at[use], dev(z, ss // NK, x, ss % NK))

    def wait_yk(use):
        drain(cy.at[use, pl.ds(0, NS - 1)], cy_r.at[use])
        drain(cy.at[use, pl.ds(0, NS - 1)], cy_s.at[use])
        tops = []
        for kk in range(NK):
            top = cy[use, kk]
            for yy in range(1, NY):
                top = jnp.maximum(top, cy[use, yy * NK + kk])
            tops.append(top)
        return jnp.concatenate(tops, axis=0)

    def product(value, matrix):
        rows_ = value.shape[0]
        high = value.astype(BF16)
        low = (value - high.astype(F32)).astype(BF16)
        both = jnp.dot(jnp.concatenate([high, low], axis=0), matrix, preferred_element_type=F32)
        return both[:rows_] + both[rows_:]

    own_partials(jnp.maximum, jnp.max, False)
    inputs[1].wait()
    inputs[2].wait()
    for a in range(2):
        dd[0, a] = dual_ref[128 * a : 128 * a + 128, :].T
        dd[1, a] = demand_ref[128 * a : 128 * a + 128, :].astype(F32).T
    inputs[3].wait()
    for c in range(4):
        pt[c] = primal_ref[128 * c : 128 * c + 128, :].T
    inputs[4].wait()
    for c in range(4):
        cost[k, c : c + 1, :] = costs_ref[128 * c : 128 * c + 128].reshape(1, 128)
    cost[k, 4:8, :] = jnp.zeros((4, 128), F32)
    for a in range(2):
        for kind in range(2):
            yd[kind, 2 * y + a] = dd[kind, a, scen(s), :]
    for c in range(4):
        px[4 * k + c] = pt[c, scen(s), :]

    first = product(jnp.concatenate([dd[0, 0], dd[0, 1]], axis=1), la[s].astype(BF16))
    for b in range(NS):
        for c in range(4):
            bp[b, c] = first[SCEN * b : SCEN * b + SCEN, 128 * c : 128 * c + 128]
    bq[s] = bp[s]
    pl.semaphore_wait(barrier, NZ - 1 + PLANE - 1)

    send_yk(0, part[1, 0:4, :])
    send_plane(0)

    for ss in s_others:
        put(bp.at[ss], bq.at[s], bp_s, bp_r, dev(z, ss // NK, x, ss % NK))

    put(
        pt.at[:, scen(2 * y + 1 - k), :], px.at[pl.ds(4 * k, 4)], pt_s, pt_r, sibling
    )
    put(cost.at[k], cost.at[k], ct_s, ct_r, sibling)
    for yy in y_others:
        put(
            dd.at[:, :, scen(yy * NK + k), :], yd.at[:, pl.ds(2 * y, 2)], dd_s, dd_r, dev(z, yy, x, k)
        )
    put(la.at[s], la.at[s], sb_s, sb_r.at[y], sibling)
    up, down = (y + 1) % NY, (y + 3) % NY

    def half(yy, n):
        return la.at[yy * NK + k, 128 * n : 128 * n + 128]

    def pass_on(yy, n, to):
        put(half(yy, n), half(yy, n), la_s, la_r.at[n, yy], dev(z, to, x, k))

    def arrived(yy, n):
        drain(half(yy, n), la_r.at[n, yy])
        put(half(yy, n), half(yy, n), sb_s, sb_r.at[yy], sibling)

    pass_on(y, 0, up)
    pass_on(y, 1, down)
    pass_on(y, 1, up)
    pass_on(y, 0, down)
    def send_z(value):
        cz[z] = value
        z_far_first(
            lambda d, zz: put(cz.at[z], cz.at[z], cz_s, cz_r, dev(zz, y, x, k))
        )

    def wait_z():
        drain(cz.at[pl.ds(0, NZ - 1)], cz_r)
        drain(cz.at[pl.ds(0, NZ - 1)], cz_s)

    def backward(h, duals, moves):
        result = product(jnp.concatenate(duals, axis=1), ab[...])
        for j in range(8):
            for q in range(2):
                g[h, 2 * j + q, 0 : W // 2, :] = result[
                    q * (W // 2) : (q + 1) * (W // 2), 128 * j : 128 * j + 128
                ]
        n = W // 16
        for i in range(16):
            g[h, i, W // 2 : SR, :] = moves[i * n : (i + 1) * n, :]
        send_parts(h)

    def send_parts(h):
        z_far_first(
            lambda d, zz: put(g.at[h, zz], rsb.at[h, d - 1], rs_s.at[h], rs_r.at[h], dev(zz, y, x, k))
        )

    def sum_and_spread(h):
        drain(rsb.at[h], rs_r.at[h])
        total = g[h, z]
        for d in range(NZ - 1):
            total = total + rsb[h, d]
        gs[h, z] = total
        z_far_first(
            lambda d, zz: put(gs.at[h, z], gs.at[h, z], ag_s.at[h], ag_r.at[h], dev(zz, y, x, k))
        )
        drain(rsb.at[h], rs_s.at[h])

    def part_of(h):
        return slice(h * W, (h + 1) * W)

    send_z(wait_yk(0))
    drain(bq.at[pl.ds(0, NS - 1)], bp_r)
    for kk in range(NK):
        total = bq[kk]
        for yy in range(1, NY):
            total = total + bq[yy * NK + kk]
        for c in range(4):
            for h in range(HALVES):
                for q in range(2):
                    top = h * W + q * (W // 2)
                    g[h, 8 * kk + 2 * c + q, 0 : W // 2, :] = total[c, top : top + W // 2, :]
    for h in range(HALVES):
        for i in range(16):
            g[h, i, W // 2 : SR, :] = jnp.zeros((W // 16, 128), F32)
        send_parts(h)
    rescale_rows(0)
    wait_z()
    csr[...] = csr[...] / jnp.sqrt(jnp.max(cz[...], axis=0) + EPSILON)
    own_partials(jnp.maximum, jnp.max, True)
    send_cols(0)
    send_plane(1)
    arrived(down, 0)
    pass_on(down, 0, up)
    arrived(up, 1)
    pass_on(up, 1, down)
    for h in range(HALVES):
        sum_and_spread(h)
    rescale_rows(1)
    wait_cols(0)
    send_yk(1, jnp.max(cz4[0], axis=0))
    csr[...] = csr[...] / jnp.sqrt(wait_yk(1) + EPSILON)
    own_partials(jnp.add, jnp.sum, True)
    send_cols(1)
    send_plane(2)
    drain(rp.at[2, pl.ds(0, PLANE - 1)], rp_r.at[2])
    drain(rp.at[2, pl.ds(0, PLANE - 1)], rp_s.at[2])
    tall = None
    for yy in range(NY):
        total = rp[2, yy]
        for cc in range(1, NX * NK):
            total = total + rp[2, cc * NY + yy]
        tall = total if tall is None else jnp.maximum(tall, total)
    tz[z, 0:1, :] = jnp.max(tall, axis=0, keepdims=True)
    tallest = tz.at[z, 0:1]
    z_far_first(lambda d, zz: put(tallest, tallest, tz_s, tz_r, dev(zz, y, x, k)))
    wait_cols(1)
    total = cz4[1, 0]
    for i in range(1, NZ):
        total = total + cz4[1, i]
    cp[slot_here] = total
    here = cp.at[slot_here]
    plane(lambda device: put(here, here, cp_s, cp_r, device))
    arrived(up, 0)
    arrived(down, 1)
    arrived((y + 2) % NY, 0)
    arrived((y + 2) % NY, 1)
    for yy in range(NY):
        drain(la.at[yy * NK + 1 - k], sb_r.at[yy])
    for b in range(8):
        ab[256 * (b // 2) : 256 * (b // 2) + 256, 512 * (b % 2) : 512 * (b % 2) + 512] = la[b].astype(BF16)
    for b in range(8):
        at[512 * (b % 2) : 512 * (b % 2) + 512, 256 * (b // 2) : 256 * (b // 2) + 256] = la[b].T.astype(BF16)
    drain(px.at[pl.ds(0, 4)], pt_r)
    drain(cost.at[0], ct_r)
    drain(yd.at[:, pl.ds(0, 6)], dd_r)
    for i in range(8):
        yd[0, i] = yd[0, i] / rsr[i : i + 1, :]
        yd[1, i] = yd[1, i] * rsr[i : i + 1, :]
        px[i] = px[i] / csr[i : i + 1, :]
    part[1] = csr[...] * jnp.concatenate([cost[0, 0:4, :], cost[1, 0:4, :]], axis=0)
    drain(cp.at[pl.ds(0, PLANE - 1)], cp_r)
    drain(cp.at[pl.ds(0, PLANE - 1)], cp_s)
    wide = None
    for cc in range(NX * NK):
        total = cp[cc * NY]
        for yy in range(1, NY):
            total = total + cp[cc * NY + yy]
        wide = total if wide is None else jnp.maximum(wide, total)
    drain(tz.at[pl.ds(0, NZ - 1), 0:1], tz_r)
    drain(tz.at[pl.ds(0, NZ - 1), 0:1], tz_s)

    def largest(tile):
        return jnp.max(jnp.max(tile, axis=1, keepdims=True), axis=0, keepdims=True)

    step_size = 0.95 / jnp.sqrt(largest(jnp.max(tz[:, 0:1, :], axis=0)) * largest(wide))

    weight = [jnp.ones((W, 1), F32) for _ in range(HALVES)]
    primal_moves = [None] * HALVES
    dual_moves = [None] * HALVES
    for t in range(ITERS):
        slot = t % 2
        last = t == ITERS - 1
        if t > 0:
            for h in range(HALVES):
                sum_and_spread(h)
        for h in range(HALVES):
            drain(gs.at[h, pl.ds(0, NZ - 1)], ag_r.at[h])
            if t > 0:
                n = W // 16
                for i in range(16):
                    mrow[h, i * n : (i + 1) * n, :] = gs[h, i, W // 2 : SR, :]
                moved = jnp.sum(mrow[h], axis=1, keepdims=True)
                weight[h] = jnp.sqrt(
                    weight[h] * jnp.sqrt((moved + EPSILON) / (primal_moves[h] + EPSILON))
                )
            rate = step_size / weight[h]
            moves, extended = jnp.zeros((W, 128), F32), []
            for j in range(8):
                scale = csr[j : j + 1, :]
                summed = jnp.concatenate(
                    [gs[h, 2 * j, 0 : W // 2, :], gs[h, 2 * j + 1, 0 : W // 2, :]], axis=0
                )
                old = px[j, part_of(h), :]
                new = jnp.maximum(old - rate * (part[1, j : j + 1, :] - scale * summed), 0.0)
                moves = moves + jnp.square(new - old)
                extended.append(scale * (2.0 * new - old))
                px[j, part_of(h), :] = new
                if last:
                    xs[j, part_of(h), :] = scale * new
            image = product(jnp.concatenate(extended, axis=1), at[...])
            for i in range(8):
                fx[slot, h, x, i] = image[:, 128 * i : 128 * i + 128]
            fx[slot, h, x, 8] = moves
            for xx in x_others:
                put(
                    fx.at[slot, h, x], fx.at[slot, h, x], fx_s.at[slot, h], fx_r.at[slot, h], dev(z, y, xx, k)
                )
            drain(gs.at[h, pl.ds(0, NZ - 1)], ag_s.at[h])
        if last:
            for c in range(4):
                solt[c, scen(s), :] = xs[4 * k + c]
            for ss in s_others:
                put(
                    xs.at[pl.ds(4 * (ss % NK), 4)], solt.at[:, scen(s), :], so_s, so_r,
                    dev(z, ss // NK, x, ss % NK),
                )
        for h in range(HALVES):
            drain(fx.at[slot, h, pl.ds(0, NX - 1)], fx_r.at[slot, h])
            rate = step_size * weight[h]
            moves, duals = jnp.zeros((W, 128), F32), []
            for i in range(8):
                scale = rsr[i : i + 1, :]
                image = fx[slot, h, 0, i] + fx[slot, h, 1, i] + fx[slot, h, 2, i] + fx[slot, h, 3, i]
                residual = yd[1, i, part_of(h), :] - scale * image
                old = yd[0, i, part_of(h), :]
                new = old + rate * residual
                moves = moves + jnp.square(new - old)
                yd[0, i, part_of(h), :] = new
                duals.append(scale * new)
                if last:
                    ydo[0, i, part_of(h), :] = scale * new
                    ydo[1, i, part_of(h), :] = residual
            primal_moves[h] = jnp.sum(
                fx[slot, h, 0, 8] + fx[slot, h, 1, 8] + fx[slot, h, 2, 8] + fx[slot, h, 3, 8],
                axis=1, keepdims=True,
            )
            if last:
                dual_moves[h] = jnp.sum(moves, axis=1, keepdims=True)
            else:
                backward(h, duals, moves)
            drain(fx.at[slot, h, pl.ds(0, NX - 1)], fx_s.at[slot, h])

    def as_row(columns):
        column = jnp.broadcast_to(jnp.concatenate(columns, axis=0), (SCEN, 128))
        return jnp.concatenate([column, jnp.zeros((128 - SCEN, 128), F32)], axis=0).T[0:1]

    mz[z, 0:1, :] = as_row(dual_moves)
    mine = mz.at[z, 0:1]
    z_far_first(lambda d, zz: put(mine, mine, mz_s, mz_r, dev(zz, y, x, k)))
    old_weight, moved_primal = as_row(weight), as_row(primal_moves)
    for a in range(2):
        for kind in range(2):
            drt[kind, a, scen(s), :] = ydo[kind, 2 * y + a]
    for ss in s_others:
        put(
            ydo.at[:, pl.ds(2 * (ss // NK), 2)], drt.at[:, :, scen(s), :], dr_s, dr_r,
            dev(z, ss // NK, x, ss % NK),
        )
    drain(solt.at[:, pl.ds(0, SCEN * (NS - 1)), :], so_r)
    for c in range(4):
        sol_ref[128 * c : 128 * c + 128, :] = solt[c].T
    outputs = [
        pltpu.make_async_copy(sol_ref, sol_hbm, out_s.at[0]),
        pltpu.make_async_copy(dv_ref, dv_hbm, out_s.at[1]),
        pltpu.make_async_copy(res_ref, res_hbm, out_s.at[2]),
    ]
    outputs[0].start()
    drain(mz.at[pl.ds(0, NZ - 1), 0:1], mz_r)
    moved = mz[0, 0:1, :]
    for i in range(1, NZ):
        moved = moved + mz[i, 0:1, :]
    wy[s, 0:1, :] = jnp.sqrt(old_weight * jnp.sqrt((moved + EPSILON) / (moved_primal + EPSILON)))
    for ss in s_others:
        put(wy.at[s, 0:1], wy.at[s, 0:1], wy_s, wy_r, dev(z, ss // NK, x, ss % NK))
    drain(drt.at[:, :, pl.ds(0, SCEN * (NS - 1)), :], dr_r)
    for a in range(2):
        dv_ref[128 * a : 128 * a + 128, :] = drt[0, a].T
        res_ref[128 * a : 128 * a + 128, :] = drt[1, a].T
    outputs[1].start()
    outputs[2].start()
    drain(wy.at[pl.ds(0, NS - 1), 0:1], wy_r)
    every = jnp.concatenate([wy[b, 0:1, :] for b in range(NS)], axis=0)
    low, high = every[0:1], every[4:5]
    for b in range(1, 4):
        moved_on = pltpu.roll(every, SCEN * b, 1)
        low, high = low + moved_on[b : b + 1], high + moved_on[4 + b : 5 + b]
    w_ref[0:128] = low.reshape(128)
    w_ref[128:256] = high.reshape(128)
    for copy in outputs:
        copy.wait()

    drain(la.at[pl.ds(0, NY - 1)], la_s)
    drain(bq.at[pl.ds(0, NS - 1)], bp_s)
    drain(la.at[pl.ds(0, NY)], sb_s)
    drain(px.at[pl.ds(0, 4)], pt_s)
    drain(cost.at[0], ct_s)
    drain(yd.at[:, pl.ds(0, 6)], dd_s)
    drain(solt.at[:, pl.ds(0, SCEN * (NS - 1)), :], so_s)
    drain(mz.at[pl.ds(0, NZ - 1), 0:1], mz_s)
    drain(drt.at[:, :, pl.ds(0, SCEN * (NS - 1)), :], dr_s)
    drain(wy.at[pl.ds(0, NS - 1), 0:1], wy_s)


def hand_over(*refs):
    sources, targets, held, sems = refs[:4], refs[4:8], refs[8:12], refs[12]
    first = [pltpu.make_async_copy(sources[i], held[i], sems.at[0, i]) for i in range(4)]
    second = [pltpu.make_async_copy(held[i], targets[i], sems.at[1, i]) for i in range(4)]
    for copy in first:
        copy.start()
    for i in (3, 1, 2, 0):
        first[i].wait()
        second[i].start()
    for copy in second:
        copy.wait()


def body(
    tile_blocks, tile_row, tile_col, tile_count, column_costs, demand, primal_start, dual_start
):
    smem = pl.BlockSpec(memory_space=pltpu.SMEM)
    vmem = pl.BlockSpec(memory_space=pltpu.VMEM)
    hbm = pl.BlockSpec(memory_space=pltpu.HBM)
    dma = pltpu.SemaphoreType.DMA
    results = pl.pallas_call(
        kernel,
        out_shape=(
            jax.ShapeDtypeStruct((512, 256), F32),
            jax.ShapeDtypeStruct((256, 256), F32),
            jax.ShapeDtypeStruct((256, 256), F32),
            jax.ShapeDtypeStruct((SCEN * NS,), F32),
        ),
        in_specs=[smem, smem, smem, hbm, hbm, hbm, hbm, hbm],
        out_specs=(hbm, hbm, hbm, vmem),
        scratch_shapes=[
            pltpu.VMEM((8, 128, 128), BF16),
            pltpu.VMEM((512,), F32),
            pltpu.VMEM((256, 256), jnp.int32),
            pltpu.VMEM((512, 256), F32),
            pltpu.VMEM((256, 256), F32),
            dma((5,)),
            pltpu.VMEM((512, 256), F32),
            pltpu.VMEM((256, 256), F32),
            pltpu.VMEM((256, 256), F32),
            dma((3,)),
            pltpu.VMEM((8, 256, 512), F32),
            pltpu.VMEM((1024, 1024), BF16),
            pltpu.VMEM((1024, 1024), BF16),
            pltpu.VMEM((2, 2, 256, 128), F32),
            pltpu.VMEM((2, 8, SCEN, 128), F32),
            pltpu.VMEM((4, 256, 128), F32),
            pltpu.VMEM((8, SCEN, 128), F32),
            pltpu.VMEM((2, 8, 128), F32),
            pltpu.VMEM((8, 128), F32),
            pltpu.VMEM((8, 128), F32),
            pltpu.VMEM((2, 8, 128), F32),
            pltpu.VMEM((NS, 4, SCEN, 128), F32),
            pltpu.VMEM((NS, 4, SCEN, 128), F32),
            pltpu.VMEM((3, PLANE, 2, 128), F32),
            pltpu.VMEM((PLANE, 4, 128), F32),
            pltpu.VMEM((2, NS, 4, 128), F32),
            pltpu.VMEM((2, NZ, 4, 128), F32),
            pltpu.VMEM((NZ, 8, 128), F32),
            pltpu.VMEM((NZ, 8, 128), F32),
            pltpu.VMEM((HALVES, NZ, SR, 128), F32),
            pltpu.VMEM((HALVES, NZ - 1, SR, 128), F32),
            pltpu.VMEM((HALVES, NZ, SR, 128), F32),
            pltpu.VMEM((HALVES, W, 128), F32),
            pltpu.VMEM((2, HALVES, NX, 9, W, 128), F32),
            pltpu.VMEM((8, SCEN, 128), F32),
            pltpu.VMEM((2, 8, SCEN, 128), F32),
            pltpu.VMEM((4, 256, 128), F32),
            pltpu.VMEM((2, 2, 256, 128), F32),
            pltpu.VMEM((NZ, 8, 128), F32),
            pltpu.VMEM((NS, 8, 128), F32),
            dma, dma,
            dma, dma((2, NY)),
            dma, dma((NY,)),
            dma, dma,
            dma, dma,
            dma, dma,
            dma((3,)), dma((3,)),
            dma, dma,
            dma((2,)), dma((2,)),
            dma((2,)), dma((2,)),
            dma, dma,
            dma, dma,
            dma((HALVES,)), dma((HALVES,)),
            dma((HALVES,)), dma((HALVES,)),
            dma((2, HALVES)), dma((2, HALVES)),
            dma, dma,
            dma, dma,
            dma, dma,
            dma, dma,
        ],
        compiler_params=pltpu.CompilerParams(
            collective_id=0, has_side_effects=True, vmem_limit_bytes=60 << 20
        ),
    )(
        tile_row, tile_col, tile_count, tile_blocks, column_costs, demand, primal_start, dual_start
    )
    return pl.pallas_call(
        hand_over,
        out_shape=tuple(jax.ShapeDtypeStruct(r.shape, F32) for r in results),
        in_specs=[hbm] * 4,
        out_specs=(hbm,) * 4,
        scratch_shapes=[pltpu.VMEM(r.shape, F32) for r in results] + [dma((2, 4))],
        compiler_params=pltpu.CompilerParams(vmem_limit_bytes=60 << 20),
    )(*results)


def solution(mesh):
    return jax.shard_map(
        body,
        mesh=mesh,
        in_specs=(
            P("rows", "cols", None, None),
            P("rows", "cols"),
            P("rows", "cols"),
            P("rows", "cols"),
            P("cols"),
            P("rows", None),
            P("cols", None),
            P("rows", None),
        ),
        out_specs=(P("cols", None), P("rows", None), P("rows", None), P()),
        check_vma=False,
    )
```

```python
import functools

import jax
import jax.numpy as jnp
from jax import lax
from jax.experimental import pallas as pl
from jax.experimental.pallas import tpu as pltpu
from jax.sharding import PartitionSpec as P

NZ, NY, NX, NK = 16, 4, 4, 2
NS = NY * NK
PLANE = NX * NY * NK
SCEN = 32
HALVES = 2
W = SCEN // HALVES
SR = W // 2 + W // 16
ITERS = 4
EPSILON = 1e-06
MESH = pl.DeviceIdType.MESH
F32, BF16 = jnp.float32, jnp.bfloat16


def kernel(
    row_ref, col_ref, count_ref, tiles_hbm, costs_hbm, demand_hbm, primal_hbm, dual_hbm,
    sol_hbm, dv_hbm, res_hbm, w_ref,
    tiles_ref, costs_ref, demand_ref, primal_ref, dual_ref, in_s, sol_ref, dv_ref, res_ref, out_s, la, ab, at, dd, yd, pt, px, cost, rsr, csr, part, bp, bq, rp, cp, cy, cz4, cz, tz, g, rsb, gs, mrow, fx, xs, ydo, solt, drt, mz, wy,
    dd_s, dd_r, la_s, la_r, sb_s, sb_r, pt_s, pt_r, ct_s, ct_r, bp_s, bp_r, rp_s, rp_r, cp_s, cp_r, cy_s, cy_r, c4_s, c4_r, cz_s, cz_r, tz_s, tz_r,
    rs_s, rs_r, ag_s, ag_r, fx_s, fx_r, so_s, so_r, dr_s, dr_r, mz_s, mz_r, wy_s, wy_r,
):
    rows, cols = lax.axis_index("rows"), lax.axis_index("cols")
    z, y, x, k = rows // NY, rows % NY, cols // NK, cols % NK
    s = y * NK + k

    def dev(zz, yy, xx, kk):
        return (zz * NY + yy, xx * NK + kk)

    def put(src, dst, ss, rs, device):
        pltpu.make_async_remote_copy(
            src_ref=src, dst_ref=dst, send_sem=ss, recv_sem=rs, device_id=device, device_id_type=MESH
        ).start()

    def drain(ref, sem):
        pltpu.make_async_copy(ref, ref, sem).wait()

    def z_far_first(send):
        def step(i, carry):
            turn = (i + 1) // 2
            d = 8 + turn - 2 * turn * (i % 2)
            send(d, (z + d) % NZ)
            return carry

        lax.fori_loop(0, NZ - 1, step, 0)

    def scen(block):
        return pl.ds(pl.multiple_of(SCEN * block, SCEN), SCEN)

    sibling = dev(z, y, x, 1 - k)
    y_others = [(y + d) % NY for d in (1, 3, 2)]
    x_others = [(x + d) % NX for d in (2, 1, 3)]
    s_others = [(s + d) % NS for d in (4, 3, 5, 2, 6, 1, 7)]

    me = y * NX * NK + cols

    def plane(send):
        def step(d, carry):
            other = (me + d) % PLANE
            send((z * NY + other // (NX * NK), other % (NX * NK)))
            return carry

        lax.fori_loop(1, PLANE, step, 0)

    barrier = pltpu.get_barrier_semaphore()

    def greet(device):
        pl.semaphore_signal(barrier, inc=1, device_id=device, device_id_type=MESH)

    z_far_first(lambda d, zz: greet(dev(zz, y, x, k)))
    plane(greet)
    inputs = [
        pltpu.make_async_copy(source, target, in_s.at[i])
        for i, (source, target) in enumerate((
            (tiles_hbm.at[0], tiles_ref), (dual_hbm, dual_ref), (demand_hbm, demand_ref),
            (primal_hbm, primal_ref), (costs_hbm, costs_ref),
        ))
    ]
    for copy in inputs:
        copy.start()

    inputs[0].wait()
    for rb in range(2):
        for cb in range(4):
            slot = jnp.int32(0)
            for t in range(8):
                same = jnp.logical_and(row_ref[0, t] == rb, col_ref[0, t] == cb)
                slot = jnp.where(same, t, slot)
            live = slot < count_ref[0, 0]
            block = tiles_ref[slot].astype(F32)
            la[s, 128 * rb : 128 * rb + 128, 128 * cb : 128 * cb + 128] = jnp.where(live, block, 0.0)
    rsr[...] = jnp.ones((8, 128), F32)
    csr[...] = jnp.ones((8, 128), F32)

    def own_partials(op, reduce, scaled):
        col_acc = [None] * 4
        for a in range(2):
            row_acc = None
            if scaled:
                row_scale = jnp.broadcast_to(rsr[pl.ds(2 * y + a, 1), :], (128, 128)).T
            for c in range(4):
                tile = jnp.abs(la[s, 128 * a : 128 * a + 128, 128 * c : 128 * c + 128])
                if scaled:
                    tile = tile * row_scale * csr[pl.ds(4 * k + c, 1), :]
                row_acc = tile if c == 0 else op(row_acc, tile)
                top = reduce(tile.reshape(16, 8, 128), axis=0)
                col_acc[c] = top if a == 0 else op(col_acc[c], top)
            part[0, a : a + 1, :] = reduce(row_acc.T, axis=0, keepdims=True)
        for c in range(4):
            part[1, c : c + 1, :] = reduce(col_acc[c], axis=0, keepdims=True)

    slot_here = cols * NY + y

    def send_plane(use):
        rp[use, slot_here] = part[0, 0:2, :]
        here = rp.at[use, slot_here]
        plane(lambda device: put(here, here, rp_s.at[use], rp_r.at[use], device))

    def send_cols(use):
        cz4[use, z] = part[1, 0:4, :]
        here = cz4.at[use, z]
        z_far_first(lambda d, zz: put(here, here, c4_s.at[use], c4_r.at[use], dev(zz, y, x, k)))

    def wait_cols(use):
        drain(cz4.at[use, pl.ds(0, NZ - 1)], c4_r.at[use])

    def rescale_rows(use):
        drain(rp.at[use, pl.ds(0, PLANE - 1)], rp_r.at[use])
        for yy in range(NY):
            top = rp[use, yy]
            for cc in range(1, NX * NK):
                top = jnp.maximum(top, rp[use, cc * NY + yy])
            both = slice(2 * yy, 2 * yy + 2)
            rsr[both, :] = rsr[both, :] / jnp.sqrt(top + EPSILON)

    def send_yk(use, value):
        cy[use, s] = value
        for ss in s_others:
            put(cy.at[use, s], cy.at[use, s], cy_s.at[use], cy_r.at[use], dev(z, ss // NK, x, ss % NK))

    def wait_yk(use):
        drain(cy.at[use, pl.ds(0, NS - 1)], cy_r.at[use])
        tops = []
        for kk in range(NK):
            top = cy[use, kk]
            for yy in range(1, NY):
                top = jnp.maximum(top, cy[use, yy * NK + kk])
            tops.append(top)
        return jnp.concatenate(tops, axis=0)

    def product(value, matrix):
        rows_ = value.shape[0]
        high = value.astype(BF16)
        low = (value - high.astype(F32)).astype(BF16)
        both = jnp.dot(jnp.concatenate([high, low], axis=0), matrix, preferred_element_type=F32)
        return both[:rows_] + both[rows_:]

    own_partials(jnp.maximum, jnp.max, False)
    inputs[1].wait()
    inputs[2].wait()
    for a in range(2):
        dd[0, a] = dual_ref[128 * a : 128 * a + 128, :].T
        dd[1, a] = demand_ref[128 * a : 128 * a + 128, :].astype(F32).T
    inputs[3].wait()
    for c in range(4):
        pt[c] = primal_ref[128 * c : 128 * c + 128, :].T
    inputs[4].wait()
    for c in range(4):
        cost[k, c : c + 1, :] = costs_ref[128 * c : 128 * c + 128].reshape(1, 128)
    cost[k, 4:8, :] = jnp.zeros((4, 128), F32)
    for a in range(2):
        for kind in range(2):
            yd[kind, 2 * y + a] = dd[kind, a, scen(s), :]
    for c in range(4):
        px[4 * k + c] = pt[c, scen(s), :]

    first = product(jnp.concatenate([dd[0, 0], dd[0, 1]], axis=1), la[s].astype(BF16))
    for b in range(NS):
        for c in range(4):
            bp[b, c] = first[SCEN * b : SCEN * b + SCEN, 128 * c : 128 * c + 128]
    bq[s] = bp[s]
    pl.semaphore_wait(barrier, NZ - 1 + PLANE - 1)

    send_yk(0, part[1, 0:4, :])
    send_plane(0)

    for ss in s_others:
        put(bp.at[ss], bq.at[s], bp_s, bp_r, dev(z, ss // NK, x, ss % NK))

    put(
        pt.at[:, scen(2 * y + 1 - k), :], px.at[pl.ds(4 * k, 4)], pt_s, pt_r, sibling
    )
    put(cost.at[k], cost.at[k], ct_s, ct_r, sibling)
    for yy in y_others:
        put(
            dd.at[:, :, scen(yy * NK + k), :], yd.at[:, pl.ds(2 * y, 2)], dd_s, dd_r, dev(z, yy, x, k)
        )
    put(la.at[s], la.at[s], sb_s, sb_r.at[y], sibling)
    up, down = (y + 1) % NY, (y + 3) % NY

    def half(yy, n):
        return la.at[yy * NK + k, 128 * n : 128 * n + 128]

    def pass_on(yy, n, to):
        put(half(yy, n), half(yy, n), la_s, la_r.at[n, yy], dev(z, to, x, k))

    def arrived(yy, n):
        drain(half(yy, n), la_r.at[n, yy])
        put(half(yy, n), half(yy, n), sb_s, sb_r.at[yy], sibling)

    pass_on(y, 0, up)
    pass_on(y, 1, down)
    pass_on(y, 1, up)
    pass_on(y, 0, down)
    def send_z(value):
        cz[z] = value
        z_far_first(
            lambda d, zz: put(cz.at[z], cz.at[z], cz_s, cz_r, dev(zz, y, x, k))
        )

    def wait_z():
        drain(cz.at[pl.ds(0, NZ - 1)], cz_r)

    def backward(h, duals, moves):
        result = product(jnp.concatenate(duals, axis=1), ab[...])
        for j in range(8):
            for q in range(2):
                g[h, 2 * j + q, 0 : W // 2, :] = result[
                    q * (W // 2) : (q + 1) * (W // 2), 128 * j : 128 * j + 128
                ]
        n = W // 16
        for i in range(16):
            g[h, i, W // 2 : SR, :] = moves[i * n : (i + 1) * n, :]
        send_parts(h)

    def send_parts(h):
        z_far_first(
            lambda d, zz: put(g.at[h, zz], rsb.at[h, d - 1], rs_s.at[h], rs_r.at[h], dev(zz, y, x, k))
        )

    def sum_and_spread(h):
        drain(rsb.at[h], rs_r.at[h])
        total = g[h, z]
        for d in range(NZ - 1):
            total = total + rsb[h, d]
        gs[h, z] = total
        z_far_first(
            lambda d, zz: put(gs.at[h, z], gs.at[h, z], ag_s.at[h], ag_r.at[h], dev(zz, y, x, k))
        )

    def part_of(h):
        return slice(h * W, (h + 1) * W)

    send_z(wait_yk(0))
    rescale_rows(0)
    wait_z()
    drain(bq.at[pl.ds(0, NS - 1)], bp_r)
    for kk in range(NK):
        total = bq[kk]
        for yy in range(1, NY):
            total = total + bq[yy * NK + kk]
        for c in range(4):
            for h in range(HALVES):
                for q in range(2):
                    top = h * W + q * (W // 2)
                    g[h, 8 * kk + 2 * c + q, 0 : W // 2, :] = total[c, top : top + W // 2, :]
    for h in range(HALVES):
        for i in range(16):
            g[h, i, W // 2 : SR, :] = jnp.zeros((W // 16, 128), F32)
        send_parts(h)
    csr[...] = csr[...] / jnp.sqrt(jnp.max(cz[...], axis=0) + EPSILON)
    own_partials(jnp.maximum, jnp.max, True)
    send_cols(0)
    send_plane(1)
    arrived(down, 0)
    pass_on(down, 0, up)
    arrived(up, 1)
    pass_on(up, 1, down)
    for h in range(HALVES):
        sum_and_spread(h)
    rescale_rows(1)
    wait_cols(0)
    send_yk(1, jnp.max(cz4[0], axis=0))
    csr[...] = csr[...] / jnp.sqrt(wait_yk(1) + EPSILON)
    own_partials(jnp.add, jnp.sum, True)
    send_cols(1)
    send_plane(2)
    drain(rp.at[2, pl.ds(0, PLANE - 1)], rp_r.at[2])
    tall = None
    for yy in range(NY):
        total = rp[2, yy]
        for cc in range(1, NX * NK):
            total = total + rp[2, cc * NY + yy]
        tall = total if tall is None else jnp.maximum(tall, total)
    tz[z, 0:1, :] = jnp.max(tall, axis=0, keepdims=True)
    tallest = tz.at[z, 0:1]
    z_far_first(lambda d, zz: put(tallest, tallest, tz_s, tz_r, dev(zz, y, x, k)))
    wait_cols(1)
    total = cz4[1, 0]
    for i in range(1, NZ):
        total = total + cz4[1, i]
    cp[slot_here] = total
    here = cp.at[slot_here]
    plane(lambda device: put(here, here, cp_s, cp_r, device))
    arrived(up, 0)
    arrived(down, 1)
    arrived((y + 2) % NY, 0)
    arrived((y + 2) % NY, 1)
    for yy in range(NY):
        drain(la.at[yy * NK + 1 - k], sb_r.at[yy])
    for b in range(8):
        ab[256 * (b // 2) : 256 * (b // 2) + 256, 512 * (b % 2) : 512 * (b % 2) + 512] = la[b].astype(BF16)
    for b in range(8):
        at[512 * (b % 2) : 512 * (b % 2) + 512, 256 * (b // 2) : 256 * (b // 2) + 256] = la[b].T.astype(BF16)
    drain(px.at[pl.ds(0, 4)], pt_r)
    drain(cost.at[0], ct_r)
    drain(yd.at[:, pl.ds(0, 6)], dd_r)
    for i in range(8):
        yd[0, i] = yd[0, i] / rsr[i : i + 1, :]
        yd[1, i] = yd[1, i] * rsr[i : i + 1, :]
        px[i] = px[i] / csr[i : i + 1, :]
    part[1] = csr[...] * jnp.concatenate([cost[0, 0:4, :], cost[1, 0:4, :]], axis=0)
    drain(cp.at[pl.ds(0, PLANE - 1)], cp_r)
    wide = None
    for cc in range(NX * NK):
        total = cp[cc * NY]
        for yy in range(1, NY):
            total = total + cp[cc * NY + yy]
        wide = total if wide is None else jnp.maximum(wide, total)
    drain(tz.at[pl.ds(0, NZ - 1), 0:1], tz_r)

    def largest(tile):
        return jnp.max(jnp.max(tile, axis=1, keepdims=True), axis=0, keepdims=True)

    step_size = 0.95 / jnp.sqrt(largest(jnp.max(tz[:, 0:1, :], axis=0)) * largest(wide))

    weight = [jnp.ones((W, 1), F32) for _ in range(HALVES)]
    primal_moves = [None] * HALVES
    dual_moves = [None] * HALVES
    for t in range(ITERS):
        slot = t % 2
        last = t == ITERS - 1
        if t > 0:
            for h in range(HALVES):
                sum_and_spread(h)
        for h in range(HALVES):
            drain(gs.at[h, pl.ds(0, NZ - 1)], ag_r.at[h])
            if t > 0:
                n = W // 16
                for i in range(16):
                    mrow[h, i * n : (i + 1) * n, :] = gs[h, i, W // 2 : SR, :]
                moved = jnp.sum(mrow[h], axis=1, keepdims=True)
                weight[h] = jnp.sqrt(
                    weight[h] * jnp.sqrt((moved + EPSILON) / (primal_moves[h] + EPSILON))
                )
            rate = step_size / weight[h]
            moves, extended = jnp.zeros((W, 128), F32), []
            for j in range(8):
                scale = csr[j : j + 1, :]
                summed = jnp.concatenate(
                    [gs[h, 2 * j, 0 : W // 2, :], gs[h, 2 * j + 1, 0 : W // 2, :]], axis=0
                )
                old = px[j, part_of(h), :]
                new = jnp.maximum(old - rate * (part[1, j : j + 1, :] - scale * summed), 0.0)
                moves = moves + jnp.square(new - old)
                extended.append(scale * (2.0 * new - old))
                px[j, part_of(h), :] = new
                if last:
                    xs[j, part_of(h), :] = scale * new
            image = product(jnp.concatenate(extended, axis=1), at[...])
            for i in range(8):
                fx[slot, h, x, i] = image[:, 128 * i : 128 * i + 128]
            fx[slot, h, x, 8] = moves
            for xx in x_others:
                put(
                    fx.at[slot, h, x], fx.at[slot, h, x], fx_s.at[slot, h], fx_r.at[slot, h], dev(z, y, xx, k)
                )
            drain(rsb.at[h], rs_s.at[h])
            drain(gs.at[h, pl.ds(0, NZ - 1)], ag_s.at[h])
        if last:
            for c in range(4):
                solt[c, scen(s), :] = xs[4 * k + c]
            for ss in s_others:
                put(
                    xs.at[pl.ds(4 * (ss % NK), 4)], solt.at[:, scen(s), :], so_s, so_r,
                    dev(z, ss // NK, x, ss % NK),
                )
        for h in range(HALVES):
            drain(fx.at[slot, h, pl.ds(0, NX - 1)], fx_r.at[slot, h])
            rate = step_size * weight[h]
            moves, duals = jnp.zeros((W, 128), F32), []
            for i in range(8):
                scale = rsr[i : i + 1, :]
                image = fx[slot, h, 0, i] + fx[slot, h, 1, i] + fx[slot, h, 2, i] + fx[slot, h, 3, i]
                residual = yd[1, i, part_of(h), :] - scale * image
                old = yd[0, i, part_of(h), :]
                new = old + rate * residual
                moves = moves + jnp.square(new - old)
                yd[0, i, part_of(h), :] = new
                duals.append(scale * new)
                if last:
                    ydo[0, i, part_of(h), :] = scale * new
                    ydo[1, i, part_of(h), :] = residual
            primal_moves[h] = jnp.sum(
                fx[slot, h, 0, 8] + fx[slot, h, 1, 8] + fx[slot, h, 2, 8] + fx[slot, h, 3, 8],
                axis=1, keepdims=True,
            )
            if last:
                dual_moves[h] = jnp.sum(moves, axis=1, keepdims=True)
            else:
                backward(h, duals, moves)
            drain(fx.at[slot, h, pl.ds(0, NX - 1)], fx_s.at[slot, h])

    def as_row(columns):
        column = jnp.broadcast_to(jnp.concatenate(columns, axis=0), (SCEN, 128))
        return jnp.concatenate([column, jnp.zeros((128 - SCEN, 128), F32)], axis=0).T[0:1]

    mz[z, 0:1, :] = as_row(dual_moves)
    mine = mz.at[z, 0:1]
    z_far_first(lambda d, zz: put(mine, mine, mz_s, mz_r, dev(zz, y, x, k)))
    old_weight, moved_primal = as_row(weight), as_row(primal_moves)
    for a in range(2):
        for kind in range(2):
            drt[kind, a, scen(s), :] = ydo[kind, 2 * y + a]
    for ss in s_others:
        put(
            ydo.at[:, pl.ds(2 * (ss // NK), 2)], drt.at[:, :, scen(s), :], dr_s, dr_r,
            dev(z, ss // NK, x, ss % NK),
        )
    drain(solt.at[:, pl.ds(0, SCEN * (NS - 1)), :], so_r)
    for c in range(4):
        sol_ref[128 * c : 128 * c + 128, :] = solt[c].T
    outputs = [
        pltpu.make_async_copy(sol_ref, sol_hbm, out_s.at[0]),
        pltpu.make_async_copy(dv_ref, dv_hbm, out_s.at[1]),
        pltpu.make_async_copy(res_ref, res_hbm, out_s.at[2]),
    ]
    outputs[0].start()
    drain(mz.at[pl.ds(0, NZ - 1), 0:1], mz_r)
    moved = mz[0, 0:1, :]
    for i in range(1, NZ):
        moved = moved + mz[i, 0:1, :]
    wy[s, 0:1, :] = jnp.sqrt(old_weight * jnp.sqrt((moved + EPSILON) / (moved_primal + EPSILON)))
    for ss in s_others:
        put(wy.at[s, 0:1], wy.at[s, 0:1], wy_s, wy_r, dev(z, ss // NK, x, ss % NK))
    drain(drt.at[:, :, pl.ds(0, SCEN * (NS - 1)), :], dr_r)
    for a in range(2):
        dv_ref[128 * a : 128 * a + 128, :] = drt[0, a].T
        res_ref[128 * a : 128 * a + 128, :] = drt[1, a].T
    outputs[1].start()
    outputs[2].start()
    drain(wy.at[pl.ds(0, NS - 1), 0:1], wy_r)
    every = jnp.concatenate([wy[b, 0:1, :] for b in range(NS)], axis=0)
    low, high = every[0:1], every[4:5]
    for b in range(1, 4):
        moved_on = pltpu.roll(every, SCEN * b, 1)
        low, high = low + moved_on[b : b + 1], high + moved_on[4 + b : 5 + b]
    w_ref[0:128] = low.reshape(128)
    w_ref[128:256] = high.reshape(128)
    for copy in outputs:
        copy.wait()

    for use in range(3):
        drain(rp.at[use, pl.ds(0, PLANE - 1)], rp_s.at[use])
    for use in range(2):
        drain(cy.at[use, pl.ds(0, NS - 1)], cy_s.at[use])
        drain(cz4.at[use, pl.ds(0, NZ - 1)], c4_s.at[use])
    drain(cz.at[pl.ds(0, NZ - 1)], cz_s)
    drain(tz.at[pl.ds(0, NZ - 1), 0:1], tz_s)
    drain(cp.at[pl.ds(0, PLANE - 1)], cp_s)
    drain(la.at[pl.ds(0, NY - 1)], la_s)
    drain(bq.at[pl.ds(0, NS - 1)], bp_s)
    drain(la.at[pl.ds(0, NY)], sb_s)
    drain(px.at[pl.ds(0, 4)], pt_s)
    drain(cost.at[0], ct_s)
    drain(yd.at[:, pl.ds(0, 6)], dd_s)
    drain(solt.at[:, pl.ds(0, SCEN * (NS - 1)), :], so_s)
    drain(mz.at[pl.ds(0, NZ - 1), 0:1], mz_s)
    drain(drt.at[:, :, pl.ds(0, SCEN * (NS - 1)), :], dr_s)
    drain(wy.at[pl.ds(0, NS - 1), 0:1], wy_s)


def hand_over(*refs):
    sources, targets, held, sems = refs[:4], refs[4:8], refs[8:12], refs[12]
    first = [pltpu.make_async_copy(sources[i], held[i], sems.at[0, i]) for i in range(4)]
    second = [pltpu.make_async_copy(held[i], targets[i], sems.at[1, i]) for i in range(4)]
    for copy in first:
        copy.start()
    for i in (3, 1, 2, 0):
        first[i].wait()
        second[i].start()
    for copy in second:
        copy.wait()


def body(
    tile_blocks, tile_row, tile_col, tile_count, column_costs, demand, primal_start, dual_start
):
    smem = pl.BlockSpec(memory_space=pltpu.SMEM)
    vmem = pl.BlockSpec(memory_space=pltpu.VMEM)
    hbm = pl.BlockSpec(memory_space=pltpu.HBM)
    dma = pltpu.SemaphoreType.DMA
    results = pl.pallas_call(
        kernel,
        out_shape=(
            jax.ShapeDtypeStruct((512, 256), F32),
            jax.ShapeDtypeStruct((256, 256), F32),
            jax.ShapeDtypeStruct((256, 256), F32),
            jax.ShapeDtypeStruct((SCEN * NS,), F32),
        ),
        in_specs=[smem, smem, smem, hbm, hbm, hbm, hbm, hbm],
        out_specs=(hbm, hbm, hbm, vmem),
        scratch_shapes=[
            pltpu.VMEM((8, 128, 128), BF16),
            pltpu.VMEM((512,), F32),
            pltpu.VMEM((256, 256), jnp.int32),
            pltpu.VMEM((512, 256), F32),
            pltpu.VMEM((256, 256), F32),
            dma((5,)),
            pltpu.VMEM((512, 256), F32),
            pltpu.VMEM((256, 256), F32),
            pltpu.VMEM((256, 256), F32),
            dma((3,)),
            pltpu.VMEM((8, 256, 512), F32),
            pltpu.VMEM((1024, 1024), BF16),
            pltpu.VMEM((1024, 1024), BF16),
            pltpu.VMEM((2, 2, 256, 128), F32),
            pltpu.VMEM((2, 8, SCEN, 128), F32),
            pltpu.VMEM((4, 256, 128), F32),
            pltpu.VMEM((8, SCEN, 128), F32),
            pltpu.VMEM((2, 8, 128), F32),
            pltpu.VMEM((8, 128), F32),
            pltpu.VMEM((8, 128), F32),
            pltpu.VMEM((2, 8, 128), F32),
            pltpu.VMEM((NS, 4, SCEN, 128), F32),
            pltpu.VMEM((NS, 4, SCEN, 128), F32),
            pltpu.VMEM((3, PLANE, 2, 128), F32),
            pltpu.VMEM((PLANE, 4, 128), F32),
            pltpu.VMEM((2, NS, 4, 128), F32),
            pltpu.VMEM((2, NZ, 4, 128), F32),
            pltpu.VMEM((NZ, 8, 128), F32),
            pltpu.VMEM((NZ, 8, 128), F32),
            pltpu.VMEM((HALVES, NZ, SR, 128), F32),
            pltpu.VMEM((HALVES, NZ - 1, SR, 128), F32),
            pltpu.VMEM((HALVES, NZ, SR, 128), F32),
            pltpu.VMEM((HALVES, W, 128), F32),
            pltpu.VMEM((2, HALVES, NX, 9, W, 128), F32),
            pltpu.VMEM((8, SCEN, 128), F32),
            pltpu.VMEM((2, 8, SCEN, 128), F32),
            pltpu.VMEM((4, 256, 128), F32),
            pltpu.VMEM((2, 2, 256, 128), F32),
            pltpu.VMEM((NZ, 8, 128), F32),
            pltpu.VMEM((NS, 8, 128), F32),
            dma, dma,
            dma, dma((2, NY)),
            dma, dma((NY,)),
            dma, dma,
            dma, dma,
            dma, dma,
            dma((3,)), dma((3,)),
            dma, dma,
            dma((2,)), dma((2,)),
            dma((2,)), dma((2,)),
            dma, dma,
            dma, dma,
            dma((HALVES,)), dma((HALVES,)),
            dma((HALVES,)), dma((HALVES,)),
            dma((2, HALVES)), dma((2, HALVES)),
            dma, dma,
            dma, dma,
            dma, dma,
            dma, dma,
        ],
        compiler_params=pltpu.CompilerParams(
            collective_id=0, has_side_effects=True, vmem_limit_bytes=60 << 20
        ),
    )(
        tile_row, tile_col, tile_count, tile_blocks, column_costs, demand, primal_start, dual_start
    )
    return pl.pallas_call(
        hand_over,
        out_shape=tuple(jax.ShapeDtypeStruct(r.shape, F32) for r in results),
        in_specs=[hbm] * 4,
        out_specs=(hbm,) * 4,
        scratch_shapes=[pltpu.VMEM(r.shape, F32) for r in results] + [dma((2, 4))],
        compiler_params=pltpu.CompilerParams(vmem_limit_bytes=60 << 20),
    )(*results)


def solution(mesh):
    return jax.shard_map(
        body,
        mesh=mesh,
        in_specs=(
            P("rows", "cols", None, None),
            P("rows", "cols"),
            P("rows", "cols"),
            P("rows", "cols"),
            P("cols"),
            P("rows", None),
            P("cols", None),
            P("rows", None),
        ),
        out_specs=(P("cols", None), P("rows", None), P("rows", None), P()),
        check_vma=False,
    )
```
